512 devices in a mesh: tok: 32 (over y, x, core), proto: 16 (over z).
Axes of the slice: x: 4, y: 4, z: 16, core: 2. Of those that a mesh axis runs over, the one named last changes fastest.
Arguments:
- patches: bfloat16 [32768, 256], P(('tok', 'proto'))
- mask_index: int32 [16384], P('tok'), may hold values from 0 to 32767, as said below
- proto_weight: float32 [256, 65536], P('tok', 'proto')
Outputs:
- targets: bfloat16 [16384, 65536], P('tok', 'proto')
The draws below stay inside these ranges and needn't reach their ends.
Inputs may be any that keep to these rules, and one draw needn't show every extreme that they name: mask_index holds distinct values; the value at position i lies in [(i // 512) * 1024, (i // 512 + 1) * 1024).
All inputs are finite; a program needn't handle non-finite values.
Results may differ from the reference program's by a relative error of at most 0.0072.
Values may be sent and summed in bfloat16 or wider, within the bound.
A program may use at most 64 MiB of HBM per device.

```python
import jax
import jax.numpy as jnp
from jax import lax

D = 256
K = 65536
TOK_DEV = 512
ITERS = 3
PATCH_GRP = 1024
MASKED = 16384
PATCHES = 32768


cluster_count = 16


def shared_centres(key):
    centre_key = jax.random.fold_in(key, 5)
    return jax.random.normal(centre_key, (cluster_count, D), jnp.float32)


def cluster_labels(key, count):
    weight_key, ticket_key = jax.random.split(key)
    weights = jax.random.randint(weight_key, (cluster_count,), 1, 11, dtype=jnp.int32)
    bounds = jnp.cumsum(weights).astype(jnp.int32)
    tickets = jax.random.randint(ticket_key, (count,), 0, bounds[cluster_count - 1], dtype=jnp.int32)
    return jnp.sum((tickets[:, None] >= bounds[None, :]).astype(jnp.int32), axis=1).astype(jnp.int32)


def image_labels(key):
    images = PATCHES // PATCH_GRP
    pair_key, pick_key = jax.random.split(key)
    cluster_pair = jax.random.randint(pair_key, (images, 2), 0, cluster_count, dtype=jnp.int32)
    row_pick = jax.random.randint(pick_key, (images, PATCH_GRP), 0, 2, dtype=jnp.int32)
    labels = jnp.where(row_pick == 0, cluster_pair[:, 0:1], cluster_pair[:, 1:2])
    return labels.reshape(PATCHES).astype(jnp.int32)


def draw_patches(key, part):
    centres = shared_centres(key)
    key = jax.random.fold_in(key, 11)
    label_key, noise_key = jax.random.split(key, 2)
    labels = image_labels(label_key)
    noise = jax.random.normal(noise_key, (PATCHES, D), jnp.float32)
    pull = 0.4
    rows = pull * jnp.take(centres, labels, axis=0) + noise
    return rows.astype(jnp.bfloat16)


def draw_proto_weight(key, part):
    centres = shared_centres(key)
    key = jax.random.fold_in(key, 31)
    label_key, noise_key = jax.random.split(key)
    labels = jnp.sort(cluster_labels(label_key, K)).astype(jnp.int32)
    noise = jax.random.normal(noise_key, (K, D), jnp.float32)
    pull = 0.4
    columns = pull * jnp.take(centres, labels, axis=0) + noise
    return (columns.T * D ** (-0.5)).astype(jnp.float32)


def pick_block(block_key):
    inner_key, order_key = jax.random.split(block_key)
    inner = 1 + jax.random.permutation(inner_key, PATCH_GRP - 2)[:TOK_DEV - 2].astype(jnp.int32)
    ends = jnp.array([0, PATCH_GRP - 1], dtype=jnp.int32)
    picked = jnp.concatenate([ends, inner]).astype(jnp.int32)
    order = jax.random.permutation(order_key, TOK_DEV)
    return picked[order].astype(jnp.int32)


def draw_mask_index(key, part):
    key = jax.random.fold_in(key, 23)
    blocks = MASKED // TOK_DEV
    block_keys = jax.random.split(key, blocks)
    chosen = jax.vmap(pick_block)(block_keys)
    offsets = jnp.arange(blocks, dtype=jnp.int32)[:, None] * PATCH_GRP
    return (chosen.astype(jnp.int32) + offsets).reshape(MASKED).astype(jnp.int32)


def setup_inputs(seed: int = 0) -> dict:
    key_list = jax.random.split(jax.random.key(seed), 4)
    patches = draw_patches(jax.random.fold_in(key_list[3], 71), 0)
    mask_index = draw_mask_index(jax.random.fold_in(key_list[3], 71), 0)
    proto_weight = draw_proto_weight(jax.random.fold_in(key_list[3], 71), 0)
    return dict(patches=patches, mask_index=mask_index, proto_weight=proto_weight)


teacher_temp = 0.04

def exponent_block(feature_block, normed):
    scores = jnp.dot(feature_block, normed, preferred_element_type=jnp.float32)
    return jnp.exp(scores / teacher_temp)

def reference(patches, mask_index, proto_weight):
    selected = patches[mask_index].astype(jnp.float32)
    features = (selected * lax.rsqrt(lax.optimization_barrier(jnp.sum(selected * selected, axis=1, keepdims=True)) + 1e-06)).astype(jnp.bfloat16)
    normed = (proto_weight * lax.rsqrt(lax.optimization_barrier(jnp.sum(proto_weight * proto_weight, axis=0, keepdims=True)) + 1e-06)).astype(jnp.bfloat16)
    blocks = MASKED // TOK_DEV
    feature_blocks = features.reshape(blocks, TOK_DEV, D)
    row_scale = jnp.ones((blocks, TOK_DEV), jnp.float32)
    col_scale = jnp.ones((K,), jnp.float32)
    for step in range(ITERS):

        def add_columns(total, inputs):
            block_rows, scale_rows = inputs
            expo = exponent_block(block_rows, normed)
            return (total + lax.optimization_barrier(jnp.sum(expo * scale_rows[:, None], axis=0)), None)
        col_total, _ = lax.scan(add_columns, jnp.zeros((K,), jnp.float32), (feature_blocks, row_scale))
        col_scale = 1.0 / col_total

        def row_sum(block_rows):
            expo = exponent_block(block_rows, normed)
            return lax.optimization_barrier(jnp.sum(expo * col_scale[None, :], axis=1))
        row_scale = 1.0 / lax.map(row_sum, feature_blocks)

    def finish(inputs):
        block_rows, scale_rows = inputs
        expo = exponent_block(block_rows, normed)
        return (K * (expo * scale_rows[:, None]) * col_scale[None, :]).astype(jnp.bfloat16)
    return lax.map(finish, (feature_blocks, row_scale)).reshape(MASKED, K)
```

```python
import functools
import math

import jax
import jax.numpy as jnp
from jax import lax
from jax.experimental import pallas as pl
from jax.experimental.pallas import tpu as pltpu
from jax.sharding import PartitionSpec as P

ITERS = 3
EPS = 1e-06
TEMP = 0.04
MESH = pl.DeviceIdType.MESH
F32 = jnp.float32
BF16 = jnp.bfloat16


def far_first(n):
    return sorted(range(1, n), key=lambda d: -min(d, n - d))


def kernel(
    side, depth,
    patches_hbm, index_hbm, weight_hbm,
    expo, row_bcast, col_scale,
    patches_ref, index_ref, weight_ref,
    gathered, onehot, features, wrows, ss_own, ss_a, ss_y, normed,
    row_acc, col_a, col_b, row_x,
    load_sem, ring_send, ring_recv, w_send, w_recv, ss_send, ss_recv,
    n1_send, n1_recv, n2_send, n2_recv, share_send, share_recv,
    a_send, a_recv, b_send, b_recv, r_send, r_recv,
):
    t = lax.axis_index("tok")
    z = lax.axis_index("proto")
    core = lax.rem(t, 2)
    chip = t // 2
    x = lax.rem(chip, side)
    y = chip // side
    q = lax.rem(t, 2 * side)
    sibling = (t + 1 - 2 * core, z)
    tokens, columns = expo.shape
    half = columns // 2
    group = columns // 8
    part = half // 8
    block, width = patches_ref.shape

    def at_z(d):
        return (t, lax.rem(z + d, depth))

    def at_q(d):
        return (y * (2 * side) + lax.rem(q + d, 2 * side), z)

    def at_x(d):
        return ((y * side + lax.rem(x + d, side)) * 2 + core, z)

    def at_y(d):
        return (lax.rem(y + d, side) * (2 * side) + q, z)

    def push(src, dst, send, recv, device):
        copy = pltpu.make_async_remote_copy(
            src_ref=src, dst_ref=dst, send_sem=send, recv_sem=recv,
            device_id=device, device_id_type=MESH,
        )
        copy.start()
        return copy

    def arrived(ref, sem):
        pltpu.make_async_copy(ref, ref, sem).wait()

    def exchange(buf, n, device, send, recv):
        for d in far_first(n):
            push(buf.at[0], buf.at[d], send, recv, device(d))

    def settle(buf, n, recv):
        arrived(buf.at[pl.ds(1, n - 1)], recv)

    barrier = pltpu.get_barrier_semaphore()
    partners = (
        [at_z(1), at_z(depth - 1)]
        + [at_q(d) for d in range(1, 2 * side)]
        + [at_y(d) for d in range(1, side)]
    )
    for device in partners:
        pl.semaphore_signal(barrier, inc=1, device_id=device, device_id_type=MESH)

    loads = [
        pltpu.make_async_copy(src, dst, load_sem.at[i])
        for i, (src, dst) in enumerate((
            (weight_hbm, weight_ref), (patches_hbm, patches_ref), (index_hbm, index_ref)))
    ]
    for load in loads:
        load.start()

    loads[0].wait()
    square = jnp.sum(weight_ref[...] * weight_ref[...], axis=0, keepdims=True)
    for h in range(2):
        for k in range(8):
            lane = h * half + k * part
            ss_own[h, k:k + 1, :] = square[:, lane:lane + part]
    ss_a[0] = ss_own[core]
    own_half = pl.ds(pl.multiple_of(core * half, half), half)
    other_half = pl.ds(pl.multiple_of((1 - core) * half, half), half)
    wrows[core] = weight_ref[:, own_half]

    loads[1].wait()
    loads[2].wait()
    rows = patches_ref[...].astype(F32)
    norm = lax.rsqrt(jnp.sum(rows * rows, axis=1, keepdims=True) + EPS)
    own = pl.ds(pl.multiple_of(z * block, block), block)
    gathered[own, :] = (rows * norm).astype(BF16)

    pl.semaphore_wait(barrier, len(partners))

    for d in far_first(2 * side):
        push(ss_own.at[lax.rem(q + d, 2)], ss_a.at[d], ss_send.at[0], ss_recv.at[0], at_q(d))

    right_steps, left_steps = depth // 2, depth // 2 - 1

    def ring_slot(owner):
        owner = lax.rem(owner + depth, depth)
        return gathered.at[pl.ds(pl.multiple_of(owner * block, block), block)]

    def ring_step(s):
        if s < right_steps:
            if s >= 1:
                arrived(ring_slot(z - s), ring_recv.at[0, s - 1])
            push(ring_slot(z - s), ring_slot(z - s), ring_send.at[0, s],
                 ring_recv.at[0, s], at_z(1))
        if s < left_steps:
            if s >= 1:
                arrived(ring_slot(z + s), ring_recv.at[1, s - 1])
            push(ring_slot(z + s), ring_slot(z + s), ring_send.at[1, s],
                 ring_recv.at[1, s], at_z(depth - 1))

    ring_step(0)

    push(weight_ref.at[:, other_half], wrows.at[core], w_send, w_recv, sibling)

    for j in range(tokens // 128):
        local = (index_ref[j:j + 1, :] - t * (block * depth)).astype(F32)
        column = jnp.broadcast_to(local, (128, 128)).T
        for k in range(block * depth // 128):
            lane = lax.broadcasted_iota(jnp.int32, (128, 128), 1).astype(F32) + 128 * k
            onehot[128 * j:128 * (j + 1), 128 * k:128 * (k + 1)] = jnp.where(
                column == lane, 1.0, 0.0).astype(BF16)

    ring_step(1)
    settle(ss_a, 2 * side, ss_recv.at[0])
    ss_y[0] = jnp.sum(ss_a[...], axis=0)
    exchange(ss_y, side, at_y, ss_send.at[1], ss_recv.at[1])
    ring_step(2)
    ring_step(3)
    arrived(wrows.at[1 - core], w_recv)
    settle(ss_y, side, ss_recv.at[1])
    inverse = lax.rsqrt(jnp.sum(ss_y[...], axis=0) + EPS)
    for k in range(8):
        value = wrows[:, :, k * part:(k + 1) * part].reshape(2 * wrows.shape[1], part)
        lane = (k % 2) * part
        normed[core, k // 4, (k // 2) % 2, y, x, :, lane:lane + part] = (
            value * inverse[k:k + 1, :]).astype(BF16)

    gather = []
    for d in far_first(side):
        gather.append(push(normed.at[core, 0, :, y, x], normed.at[core, 0, :, y, x],
                           n1_send.at[0, d], n1_recv.at[0, d], at_x(d)))
        gather.append(push(normed.at[core, 1, :, y, x], normed.at[core, 1, :, y, x],
                           n1_send.at[1, d], n1_recv.at[1, d], at_y(d)))
    ring_step(4)
    ring_step(5)
    for d in range(1, side):
        px, py = lax.rem(x - d + side, side), lax.rem(y - d + side, side)
        arrived(normed.at[core, 0, :, y, px], n1_recv.at[0, d])
        arrived(normed.at[core, 1, :, py, x], n1_recv.at[1, d])
    for c in range(2):
        for d in far_first(side):
            gather.append(push(normed.at[core, 0, c, y], normed.at[core, 0, c, y],
                               n2_send.at[0, c, d], n2_recv.at[0, c, d], at_y(d)))
            gather.append(push(normed.at[core, 1, c, :, x], normed.at[core, 1, c, :, x],
                               n2_send.at[1, c, d], n2_recv.at[1, c, d], at_x(d)))
    for s in range(6, right_steps):
        ring_step(s)
    arrived(ring_slot(z - right_steps), ring_recv.at[0, right_steps - 1])
    arrived(ring_slot(z + left_steps), ring_recv.at[1, left_steps - 1])
    features[...] = jnp.dot(onehot[...], gathered[...],
                            preferred_element_type=F32).astype(BF16)

    factor = math.log2(math.e) / TEMP
    step_lanes = min(256, group)

    def fill(which, c):
        def chunk(i, carry):
            p = i // (group // step_lanes)
            start = pl.multiple_of(lax.rem(i, group // step_lanes) * step_lanes, step_lanes)
            lanes = pl.ds(start, step_lanes)
            weights = normed[which, p, c, :, :, :, lanes].reshape(width, step_lanes)
            row = which * 4 + p * 2 + c
            target = pl.ds(pl.multiple_of(row * group + start, step_lanes), step_lanes)
            scores = jnp.dot(features[...], weights, preferred_element_type=F32)
            value = jnp.exp2(scores * factor)
            expo[:, target] = value
            total = jnp.sum(value.reshape(tokens // 8, 8, step_lanes), axis=0)
            col_a[0, 0, pl.ds(row, 1), lanes] = jnp.sum(total, axis=0, keepdims=True)
            return carry

        lax.fori_loop(0, 2 * (group // step_lanes), chunk, 0)

    for c in range(2):
        for d in range(1, side):
            px, py = lax.rem(x - d + side, side), lax.rem(y - d + side, side)
            arrived(normed.at[core, 0, c, py], n2_recv.at[0, c, d])
            arrived(normed.at[core, 1, c, :, px], n2_recv.at[1, c, d])
        gather.append(push(normed.at[core, :, c], normed.at[core, :, c],
                           share_send.at[c], share_recv.at[c], sibling))
        fill(core, c)
    for c in range(2):
        arrived(normed.at[1 - core, :, c], share_recv.at[c])
        fill(1 - core, c)

    def columns_to_scale(it):
        exchange(col_a.at[it], 2 * side, at_q, a_send.at[it], a_recv.at[it])
        settle(col_a.at[it], 2 * side, a_recv.at[it])
        col_b[it, 0] = jnp.sum(col_a[it], axis=0)
        exchange(col_b.at[it], side, at_y, b_send.at[it], b_recv.at[it])
        settle(col_b.at[it], side, b_recv.at[it])
        col_scale[...] = 1.0 / jnp.sum(col_b[it], axis=0)

    def row_pass(it):
        def some(g, carry):
            here = pl.ds(pl.multiple_of(g * 64, 64), 64)
            total = jnp.zeros((64, 128), F32)
            for j in range(columns // 128):
                k, l = j // (group // 128), j % (group // 128)
                scale = col_scale[k:k + 1, 128 * l:128 * (l + 1)]
                total += expo[here, 128 * j:128 * (j + 1)] * scale
            row_acc[here, :] = total
            return carry

        lax.fori_loop(0, tokens // 64, some, 0)
        for j in range(tokens // 128):
            turned = row_acc[128 * j:128 * (j + 1), :].T
            row_x[it, 0, j:j + 1, :] = jnp.sum(turned, axis=0, keepdims=True)

    def rows_to_scale(it):
        exchange(row_x.at[it], depth, at_z, r_send.at[it], r_recv.at[it])
        settle(row_x.at[it], depth, r_recv.at[it])
        scale = 1.0 / jnp.sum(row_x[it], axis=0)
        for j in range(tokens // 128):
            row_bcast[128 * j:128 * (j + 1), :] = jnp.broadcast_to(
                scale[j:j + 1, :], (128, 128)).T

    def column_pass(it):
        def chunk(k, carry):
            target = pl.ds(pl.multiple_of(k * group, group), group)

            total = jnp.zeros((8, group), F32)
            for g in range(tokens // 64):
                here = slice(g * 64, (g + 1) * 64)
                scale = jnp.concatenate([row_bcast[here, :]] * (group // 128), axis=1)
                value = expo[here, target] * scale
                total += jnp.sum(value.reshape(8, 8, group), axis=0)
            col_a[it, 0, pl.ds(k, 1), :] = jnp.sum(total, axis=0, keepdims=True)
            return carry

        lax.fori_loop(0, 8, chunk, 0)

    def sinkhorn(it, carry):
        columns_to_scale(it)
        row_pass(it)
        rows_to_scale(it)
        column_pass(it + 1)
        return carry

    lax.fori_loop(0, ITERS - 1, sinkhorn, 0)
    columns_to_scale(ITERS - 1)
    row_pass(ITERS - 1)
    rows_to_scale(ITERS - 1)

    pltpu.make_async_copy(wrows.at[core], wrows.at[core], w_send).wait()
    for s in range(right_steps):
        arrived(ring_slot(z - s), ring_send.at[0, s])
    for s in range(left_steps):
        arrived(ring_slot(z + s), ring_send.at[1, s])
    for copy in gather:
        copy.wait_send()
    settle(ss_a, 2 * side, ss_send.at[0])
    settle(ss_y, side, ss_send.at[1])
    for it in range(ITERS):
        settle(col_a.at[it], 2 * side, a_send.at[it])
        settle(col_b.at[it], side, b_send.at[it])
        settle(row_x.at[it], depth, r_send.at[it])


def finish_kernel(scale_out, expo, row_bcast, col_scale, out_ref, staged, sems):
    tokens, columns = expo.shape
    group = columns // 8
    step = staged.shape[1]
    copies = []
    for g in range(tokens // step):
        here = slice(g * step, (g + 1) * step)
        scale = jnp.concatenate([row_bcast[here, :]] * (group // 128), axis=1)
        for k in range(8):
            target = slice(k * group, (k + 1) * group)
            value = scale_out * (expo[here, target] * scale)
            staged[g, :, target] = (value * col_scale[k:k + 1, :]).astype(BF16)
        copies.append(pltpu.make_async_copy(staged.at[g], out_ref.at[pl.ds(g * step, step)],
                                            sems.at[g]))
        copies[-1].start()
    for copy in copies:
        copy.wait()


def body(side, depth, patches, mask_index, proto_weight):
    block, width = patches.shape
    tokens = mask_index.shape[0]
    rows, columns = proto_weight.shape
    half, group = columns // 2, columns // 8
    dma = pltpu.SemaphoreType.DMA
    vmem = pl.BlockSpec(memory_space=pltpu.VMEM)
    hbm = pl.BlockSpec(memory_space=pltpu.HBM)
    expo, row_bcast, col_scale = pl.pallas_call(
        functools.partial(kernel, side, depth),
        out_shape=(
            jax.ShapeDtypeStruct((tokens, columns), F32),
            jax.ShapeDtypeStruct((tokens, 128), F32),
            jax.ShapeDtypeStruct((8, group), F32),
        ),
        in_specs=[hbm] * 3,
        out_specs=(vmem,) * 3,
        scratch_shapes=[
            pltpu.VMEM((block, width), BF16),
            pltpu.VMEM((tokens // 128, 128), jnp.int32),
            pltpu.VMEM((rows, columns), F32),
            pltpu.VMEM((block * depth, width), BF16),
            pltpu.VMEM((tokens, block * depth), BF16),
            pltpu.VMEM((tokens, width), BF16),
            pltpu.VMEM((2, rows, half), F32),
            pltpu.VMEM((2, 8, half // 8), F32),
            pltpu.VMEM((2 * side, 8, half // 8), F32),
            pltpu.VMEM((side, 8, half // 8), F32),
            pltpu.VMEM((2, 2, 2, side, side, 2 * rows, group), BF16),
            pltpu.VMEM((tokens, 128), F32),
            pltpu.VMEM((ITERS, 2 * side, 8, group), F32),
            pltpu.VMEM((ITERS, side, 8, group), F32),
            pltpu.VMEM((ITERS, depth, tokens // 128, 128), F32),
            dma((3,)),
            dma((2, depth // 2)), dma((2, depth // 2)),
            dma, dma,
            dma((2,)), dma((2,)),
            dma((2, side)), dma((2, side)),
            dma((2, 2, side)), dma((2, 2, side)),
            dma((2,)), dma((2,)),
            dma((ITERS,)), dma((ITERS,)),
            dma((ITERS,)), dma((ITERS,)),
            dma((ITERS,)), dma((ITERS,)),
        ],
        compiler_params=pltpu.CompilerParams(
            collective_id=0, has_side_effects=True,
            vmem_limit_bytes=32 * 1024 * 1024,
        ),
        cost_estimate=pl.CostEstimate(
            flops=2 * tokens * columns * width, bytes_accessed=4 * tokens * columns,
            transcendentals=tokens * columns),
    )(*(pltpu.with_memory_space_constraint(v, pltpu.HBM) for v in (
        patches, mask_index.reshape(tokens // 128, 128), proto_weight)))
    step = 64
    return pl.pallas_call(
        functools.partial(finish_kernel, float(columns * depth)),
        out_shape=jax.ShapeDtypeStruct((tokens, columns), BF16),
        in_specs=[vmem] * 3,
        out_specs=hbm,
        scratch_shapes=[pltpu.VMEM((tokens // step, step, columns), BF16),
                        dma((tokens // step,))],
        compiler_params=pltpu.CompilerParams(vmem_limit_bytes=16 * 1024 * 1024),
        cost_estimate=pl.CostEstimate(
            flops=3 * tokens * columns, bytes_accessed=6 * tokens * columns, transcendentals=0),
    )(expo, row_bcast, col_scale)


def solution(mesh):
    side = math.isqrt(mesh.shape["tok"] // 2)
    return jax.shard_map(
        functools.partial(body, side, mesh.shape["proto"]),
        mesh=mesh,
        in_specs=(P(("tok", "proto"), None), P("tok"), P("tok", "proto")),
        out_specs=P("tok", "proto"),
        check_vma=False,
    )
```

```python
import functools
import math

import jax
import jax.numpy as jnp
from jax import lax
from jax.experimental import pallas as pl
from jax.experimental.pallas import tpu as pltpu
from jax.sharding import PartitionSpec as P

ITERS = 3
EPS = 1e-06
TEMP = 0.04
MESH = pl.DeviceIdType.MESH
F32 = jnp.float32
BF16 = jnp.bfloat16


def far_first(n):
    return sorted(range(1, n), key=lambda d: -min(d, n - d))


def kernel(
    side, depth,
    patches_hbm, index_hbm, weight_hbm,
    expo, row_bcast, col_scale,
    patches_ref, index_ref, weight_ref,
    gathered, onehot, features, wrows, ss_own, ss_a, ss_y, normed,
    row_acc, col_a, col_b, row_x,
    load_sem, ring_send, ring_recv, w_send, w_recv, ss_send, ss_recv,
    n1_send, n1_recv, n2_send, n2_recv, share_send, share_recv,
    a_send, a_recv, b_send, b_recv, r_send, r_recv,
):
    t = lax.axis_index("tok")
    z = lax.axis_index("proto")
    core = lax.rem(t, 2)
    chip = t // 2
    x = lax.rem(chip, side)
    y = chip // side
    q = lax.rem(t, 2 * side)
    sibling = (t + 1 - 2 * core, z)
    tokens, columns = expo.shape
    half = columns // 2
    group = columns // 8
    part = half // 8
    block, width = patches_ref.shape

    def at_z(d):
        return (t, lax.rem(z + d, depth))

    def at_q(d):
        return (y * (2 * side) + lax.rem(q + d, 2 * side), z)

    def at_qy(d):
        to = lax.rem(y * 2 + core + d, 2 * side)
        return ((to // 2) * (2 * side) + x * 2 + lax.rem(to, 2), z)

    def at_x(d):
        return ((y * side + lax.rem(x + d, side)) * 2 + core, z)

    def at_y(d):
        return (lax.rem(y + d, side) * (2 * side) + q, z)

    def push(src, dst, send, recv, device):
        copy = pltpu.make_async_remote_copy(
            src_ref=src, dst_ref=dst, send_sem=send, recv_sem=recv,
            device_id=device, device_id_type=MESH,
        )
        copy.start()
        return copy

    def arrived(ref, sem):
        pltpu.make_async_copy(ref, ref, sem).wait()

    def exchange(buf, n, device, send, recv):
        for d in far_first(n):
            push(buf.at[0], buf.at[d], send, recv, device(d))

    def settle(buf, n, recv):
        arrived(buf.at[pl.ds(1, n - 1)], recv)

    barrier = pltpu.get_barrier_semaphore()
    partners = (
        [at_z(1), at_z(2), at_z(depth - 1), at_z(depth - 2)]
        + [at_q(d) for d in range(1, 2 * side)]
        + [at_qy(d) for d in range(1, 2 * side)]
    )
    for device in partners:
        pl.semaphore_signal(barrier, inc=1, device_id=device, device_id_type=MESH)

    loads = [
        pltpu.make_async_copy(src, dst, load_sem.at[i])
        for i, (src, dst) in enumerate((
            (weight_hbm, weight_ref), (patches_hbm, patches_ref), (index_hbm, index_ref)))
    ]
    for load in loads:
        load.start()

    loads[0].wait()
    square = jnp.sum(weight_ref[...] * weight_ref[...], axis=0, keepdims=True)
    for h in range(2):
        for k in range(8):
            lane = h * half + k * part
            ss_own[h, k:k + 1, :] = square[:, lane:lane + part]
    ss_a[0] = ss_own[core]
    own_half = pl.ds(pl.multiple_of(core * half, half), half)
    other_half = pl.ds(pl.multiple_of((1 - core) * half, half), half)
    wrows[core] = weight_ref[:, own_half]

    loads[1].wait()
    loads[2].wait()
    rows = patches_ref[...].astype(F32)
    norm = lax.rsqrt(jnp.sum(rows * rows, axis=1, keepdims=True) + EPS)
    own = pl.ds(pl.multiple_of(z * block, block), block)
    gathered[own, :] = (rows * norm).astype(BF16)

    pl.semaphore_wait(barrier, len(partners))

    for d in far_first(2 * side):
        push(ss_own.at[lax.rem(q + d, 2)], ss_a.at[d], ss_send.at[0], ss_recv.at[0], at_q(d))

    reach = (depth // 2, depth - 1 - depth // 2)

    def ring_slot(way, d):
        owner = lax.rem(z - d + depth, depth) if way == 0 else lax.rem(z + d, depth)
        return gathered.at[pl.ds(pl.multiple_of(owner * block, block), block)]

    def ring_push(way, d, hops):
        slot = ring_slot(way, d)
        push(slot, slot, ring_send.at[way, d + hops], ring_recv.at[way, d + hops],
             at_z(hops if way == 0 else depth - hops))

    def ring_step(s):
        for way in range(2):
            if s == 0:
                ring_push(way, 0, 2)
                ring_push(way, 0, 1)
        for d in (2 * s - 1, 2 * s):
            for way in range(2):
                if 1 <= d <= reach[way]:
                    arrived(ring_slot(way, d), ring_recv.at[way, d])
                    if d + 2 <= reach[way]:
                        ring_push(way, d, 2)

    ring_steps = depth // 4

    ring_step(0)

    push(weight_ref.at[:, other_half], wrows.at[core], w_send, w_recv, sibling)

    for j in range(tokens // 128):
        local = (index_ref[j:j + 1, :] - t * (block * depth)).astype(F32)
        column = jnp.broadcast_to(local, (128, 128)).T
        for k in range(block * depth // 128):
            lane = lax.broadcasted_iota(jnp.int32, (128, 128), 1).astype(F32) + 128 * k
            onehot[128 * j:128 * (j + 1), 128 * k:128 * (k + 1)] = jnp.where(
                column == lane, 1.0, 0.0).astype(BF16)

    ring_step(1)
    settle(ss_a, 2 * side, ss_recv.at[0])
    ss_y[0] = jnp.sum(ss_a[...], axis=0)
    exchange(ss_y, side, at_y, ss_send.at[1], ss_recv.at[1])
    ring_step(2)
    arrived(wrows.at[1 - core], w_recv)
    settle(ss_y, side, ss_recv.at[1])
    inverse = lax.rsqrt(jnp.sum(ss_y[...], axis=0) + EPS)
    for k in range(8):
        value = wrows[:, :, k * part:(k + 1) * part].reshape(2 * wrows.shape[1], part)
        lane = (k % 2) * part
        normed[core, k // 4, (k // 2) % 2, y, x, :, lane:lane + part] = (
            value * inverse[k:k + 1, :]).astype(BF16)

    gather = []
    for d in far_first(side):
        gather.append(push(normed.at[core, 0, :, y, x], normed.at[core, 0, :, y, x],
                           n1_send.at[0, d], n1_recv.at[0, d], at_x(d)))
        gather.append(push(normed.at[core, 1, :, y, x], normed.at[core, 1, :, y, x],
                           n1_send.at[1, d], n1_recv.at[1, d], at_y(d)))
    ring_step(3)
    for d in range(1, side):
        px, py = lax.rem(x - d + side, side), lax.rem(y - d + side, side)
        arrived(normed.at[core, 0, :, y, px], n1_recv.at[0, d])
        arrived(normed.at[core, 1, :, py, x], n1_recv.at[1, d])
    for c in range(2):
        for d in far_first(side):
            gather.append(push(normed.at[core, 0, c, y], normed.at[core, 0, c, y],
                               n2_send.at[0, c, d], n2_recv.at[0, c, d], at_y(d)))
            gather.append(push(normed.at[core, 1, c, :, x], normed.at[core, 1, c, :, x],
                               n2_send.at[1, c, d], n2_recv.at[1, c, d], at_x(d)))
    for s in range(4, ring_steps + 1):
        ring_step(s)
    features[...] = jnp.dot(onehot[...], gathered[...],
                            preferred_element_type=F32).astype(BF16)

    factor = math.log2(math.e) / TEMP
    step_lanes = min(256, group)

    def fill(which, c):
        def chunk(i, carry):
            p = i // (group // step_lanes)
            start = pl.multiple_of(lax.rem(i, group // step_lanes) * step_lanes, step_lanes)
            lanes = pl.ds(start, step_lanes)
            weights = normed[which, p, c, :, :, :, lanes].reshape(width, step_lanes)
            row = which * 4 + p * 2 + c
            target = pl.ds(pl.multiple_of(row * group + start, step_lanes), step_lanes)
            scores = jnp.dot(features[...], weights, preferred_element_type=F32)
            value = jnp.exp2(scores * factor)
            expo[:, target] = value
            total = jnp.sum(value.reshape(tokens // 8, 8, step_lanes), axis=0)
            col_a[0, which, 0, pl.ds(p * 2 + c, 1), lanes] = jnp.sum(total, axis=0, keepdims=True)
            return carry

        lax.fori_loop(0, 2 * (group // step_lanes), chunk, 0)

    def pick(h, first, second):
        return tuple(u * (1 - h) + v * h for u, v in zip(first, second))

    def column_push(it, h):
        for d in far_first(2 * side):
            push(col_a.at[it, h, 0], col_a.at[it, h, d], a_send.at[it, h], a_recv.at[it, h],
                 pick(h, at_q(d), at_qy(d)))

    for c in range(2):
        for d in range(1, side):
            px, py = lax.rem(x - d + side, side), lax.rem(y - d + side, side)
            arrived(normed.at[core, 0, c, py], n2_recv.at[0, c, d])
            arrived(normed.at[core, 1, c, :, px], n2_recv.at[1, c, d])
        gather.append(push(normed.at[core, :, c], normed.at[core, :, c],
                           share_send.at[c], share_recv.at[c], sibling))
        fill(core, c)
    column_push(0, core)
    for c in range(2):
        arrived(normed.at[1 - core, :, c], share_recv.at[c])
        fill(1 - core, c)
    column_push(0, 1 - core)

    def row_pass(h):
        def some(g, carry):
            here = pl.ds(pl.multiple_of(g * 64, 64), 64)
            total = jnp.zeros((64, 128), F32) if h == 0 else row_acc[here, :]
            for j in range(half // 128):
                k, l = j // (group // 128), j % (group // 128)
                scale = col_scale[h, k:k + 1, 128 * l:128 * (l + 1)]
                lane = h * half + 128 * j
                total += expo[here, lane:lane + 128] * scale
            row_acc[here, :] = total
            return carry

        lax.fori_loop(0, tokens // 64, some, 0)

    def columns_to_rows(it):
        for h in range(2):
            settle(col_a.at[it, h], 2 * side, a_recv.at[it, h])
            col_b[it, h, 0] = jnp.sum(col_a[it, h], axis=0)
            exchange(col_b.at[it, h], side, (at_y, at_x)[h], b_send.at[it, h], b_recv.at[it, h])
        for h in range(2):
            settle(col_b.at[it, h], side, b_recv.at[it, h])
            col_scale[h] = 1.0 / jnp.sum(col_b[it, h], axis=0)
            row_pass(h)
        for j in range(tokens // 128):
            turned = row_acc[128 * j:128 * (j + 1), :].T
            row_x[it, 0, j:j + 1, :] = jnp.sum(turned, axis=0, keepdims=True)
        exchange(row_x.at[it], depth, at_z, r_send.at[it], r_recv.at[it])

    def rows_to_scale(it):
        settle(row_x.at[it], depth, r_recv.at[it])
        scale = 1.0 / jnp.sum(row_x[it], axis=0)
        for j in range(tokens // 128):
            row_bcast[128 * j:128 * (j + 1), :] = jnp.broadcast_to(
                scale[j:j + 1, :], (128, 128)).T

    def column_pass(it, h):
        def chunk(k, carry):
            target = pl.ds(pl.multiple_of(h * half + k * group, group), group)
            total = jnp.zeros((8, group), F32)
            for g in range(tokens // 64):
                here = slice(g * 64, (g + 1) * 64)
                scale = jnp.concatenate([row_bcast[here, :]] * (group // 128), axis=1)
                value = expo[here, target] * scale
                total += jnp.sum(value.reshape(8, 8, group), axis=0)
            col_a[it, h, 0, pl.ds(k, 1), :] = jnp.sum(total, axis=0, keepdims=True)
            return carry

        lax.fori_loop(0, 4, chunk, 0)

    def sinkhorn(it, carry):
        columns_to_rows(it)
        rows_to_scale(it)
        for h in range(2):
            column_pass(it + 1, h)
            column_push(it + 1, h)
        return carry

    lax.fori_loop(0, ITERS - 1, sinkhorn, 0)
    columns_to_rows(ITERS - 1)

    pltpu.make_async_copy(wrows.at[core], wrows.at[core], w_send).wait()
    for way in range(2):
        for d in range(1, reach[way] + 1):
            arrived(ring_slot(way, d), ring_send.at[way, d])
    for copy in gather:
        copy.wait_send()
    settle(ss_a, 2 * side, ss_send.at[0])
    settle(ss_y, side, ss_send.at[1])
    for it in range(ITERS):
        for h in range(2):
            settle(col_a.at[it, h], 2 * side, a_send.at[it, h])
            settle(col_b.at[it, h], side, b_send.at[it, h])
        settle(row_x.at[it], depth, r_send.at[it])

    rows_to_scale(ITERS - 1)


def finish_kernel(scale_out, expo, row_bcast, col_scale, out_ref, staged, sems):
    tokens, columns = expo.shape
    group = columns // 8
    step = staged.shape[1]
    copies = []
    for g in range(tokens // step):
        here = slice(g * step, (g + 1) * step)
        scale = jnp.concatenate([row_bcast[here, :]] * (group // 128), axis=1)
        for k in range(8):
            target = slice(k * group, (k + 1) * group)
            value = scale_out * (expo[here, target] * scale)
            staged[g, :, target] = (value * col_scale[k // 4, k % 4:k % 4 + 1, :]).astype(BF16)
        copies.append(pltpu.make_async_copy(staged.at[g], out_ref.at[pl.ds(g * step, step)],
                                            sems.at[g]))
        copies[-1].start()
    for copy in copies:
        copy.wait()


def body(side, depth, patches, mask_index, proto_weight):
    block, width = patches.shape
    tokens = mask_index.shape[0]
    rows, columns = proto_weight.shape
    half, group = columns // 2, columns // 8
    dma = pltpu.SemaphoreType.DMA
    vmem = pl.BlockSpec(memory_space=pltpu.VMEM)
    hbm = pl.BlockSpec(memory_space=pltpu.HBM)
    expo, row_bcast, col_scale = pl.pallas_call(
        functools.partial(kernel, side, depth),
        out_shape=(
            jax.ShapeDtypeStruct((tokens, columns), F32),
            jax.ShapeDtypeStruct((tokens, 128), F32),
            jax.ShapeDtypeStruct((2, 4, group), F32),
        ),
        in_specs=[hbm] * 3,
        out_specs=(vmem,) * 3,
        scratch_shapes=[
            pltpu.VMEM((block, width), BF16),
            pltpu.VMEM((tokens // 128, 128), jnp.int32),
            pltpu.VMEM((rows, columns), F32),
            pltpu.VMEM((block * depth, width), BF16),
            pltpu.VMEM((tokens, block * depth), BF16),
            pltpu.VMEM((tokens, width), BF16),
            pltpu.VMEM((2, rows, half), F32),
            pltpu.VMEM((2, 8, half // 8), F32),
            pltpu.VMEM((2 * side, 8, half // 8), F32),
            pltpu.VMEM((side, 8, half // 8), F32),
            pltpu.VMEM((2, 2, 2, side, side, 2 * rows, group), BF16),
            pltpu.VMEM((tokens, 128), F32),
            pltpu.VMEM((ITERS, 2, 2 * side, 4, group), F32),
            pltpu.VMEM((ITERS, 2, side, 4, group), F32),
            pltpu.VMEM((ITERS, depth, tokens // 128, 128), F32),
            dma((3,)),
            dma((2, depth // 2 + 1)), dma((2, depth // 2 + 1)),
            dma, dma,
            dma((2,)), dma((2,)),
            dma((2, side)), dma((2, side)),
            dma((2, 2, side)), dma((2, 2, side)),
            dma((2,)), dma((2,)),
            dma((ITERS, 2)), dma((ITERS, 2)),
            dma((ITERS, 2)), dma((ITERS, 2)),
            dma((ITERS,)), dma((ITERS,)),
        ],
        compiler_params=pltpu.CompilerParams(
            collective_id=0, has_side_effects=True,
            vmem_limit_bytes=32 * 1024 * 1024,
        ),
        cost_estimate=pl.CostEstimate(
            flops=2 * tokens * columns * width, bytes_accessed=4 * tokens * columns,
            transcendentals=tokens * columns),
    )(*(pltpu.with_memory_space_constraint(v, pltpu.HBM) for v in (
        patches, mask_index.reshape(tokens // 128, 128), proto_weight)))
    step = 64
    return pl.pallas_call(
        functools.partial(finish_kernel, float(columns * depth)),
        out_shape=jax.ShapeDtypeStruct((tokens, columns), BF16),
        in_specs=[vmem] * 3,
        out_specs=hbm,
        scratch_shapes=[pltpu.VMEM((tokens // step, step, columns), BF16),
                        dma((tokens // step,))],
        compiler_params=pltpu.CompilerParams(vmem_limit_bytes=16 * 1024 * 1024),
        cost_estimate=pl.CostEstimate(
            flops=3 * tokens * columns, bytes_accessed=6 * tokens * columns, transcendentals=0),
    )(expo, row_bcast, col_scale)


def solution(mesh):
    side = math.isqrt(mesh.shape["tok"] // 2)
    return jax.shard_map(
        functools.partial(body, side, mesh.shape["proto"]),
        mesh=mesh,
        in_specs=(P(("tok", "proto"), None), P("tok"), P("tok", "proto")),
        out_specs=P("tok", "proto"),
        check_vma=False,
    )
```

```python
import functools
import math

import jax
import jax.numpy as jnp
from jax import lax
from jax.experimental import pallas as pl
from jax.experimental.pallas import tpu as pltpu
from jax.sharding import PartitionSpec as P

ITERS = 3
EPS = 1e-06
TEMP = 0.04
MESH = pl.DeviceIdType.MESH
F32 = jnp.float32
BF16 = jnp.bfloat16


def far_first(n):
    return sorted(range(1, n), key=lambda d: -min(d, n - d))


def kernel(
    side, depth,
    patches_hbm, index_hbm, weight_hbm,
    expo, row_bcast, col_scale,
    patches_ref, index_ref, weight_ref,
    gathered, onehot, features, raw, ss_own, ss_a, ss_y, normed,
    row_acc, col_a, col_b, row_x,
    load_sem, ring_send, ring_recv, raw_send, raw_recv, ss_send, ss_recv,
    n2_send, n2_recv, share_send, share_recv,
    a_send, a_recv, b_send, b_recv, r_send, r_recv,
):
    t = lax.axis_index("tok")
    z = lax.axis_index("proto")
    core = lax.rem(t, 2)
    chip = t // 2
    x = lax.rem(chip, side)
    y = chip // side
    q = lax.rem(t, 2 * side)
    sibling = (t + 1 - 2 * core, z)
    tokens, columns = expo.shape
    half = columns // 2
    quarter = half // 2
    group = columns // 8
    part = half // 8
    block, width = patches_ref.shape

    def wrap(value, n):
        return jnp.where(value >= n, value - n, value)

    at_z, at_q, at_qy, at_x, at_y = {}, {}, {}, {}, {}
    flip = (core, 1 - core)
    for d in range(1, depth):
        at_z[d] = (t, wrap(z + d, depth))
    for d in range(1, 2 * side):
        at_q[d] = (y * (2 * side) + wrap(q + d, 2 * side), z)
        at_qy[d] = ((wrap(y * 2 + core + d, 2 * side) - flip[d % 2]) * side
                    + x * 2 + flip[d % 2], z)
    for d in range(1, side):
        at_x[d] = ((y * side + wrap(x + d, side)) * 2 + core, z)
        at_y[d] = (wrap(y + d, side) * (2 * side) + q, z)

    def push(src, dst, send, recv, device):
        copy = pltpu.make_async_remote_copy(
            src_ref=src, dst_ref=dst, send_sem=send, recv_sem=recv,
            device_id=device, device_id_type=MESH,
        )
        copy.start()
        return copy

    def arrived(ref, sem):
        pltpu.make_async_copy(ref, ref, sem).wait()

    def exchange(buf, n, device, send, recv):
        for d in far_first(n):
            push(buf.at[0], buf.at[d], send, recv, device[d])

    def settle(buf, n, recv):
        arrived(buf.at[pl.ds(1, n - 1)], recv)

    barrier = pltpu.get_barrier_semaphore()
    partners = (
        [at_z[d] for d in (1, 2, depth - 1, depth - 2)]
        + list(at_q.values()) + list(at_qy.values())
    )
    for device in partners:
        pl.semaphore_signal(barrier, inc=1, device_id=device, device_id_type=MESH)

    loads = [
        pltpu.make_async_copy(src, dst, load_sem.at[i])
        for i, (src, dst) in enumerate((
            (weight_hbm, weight_ref), (patches_hbm, patches_ref), (index_hbm, index_ref)))
    ]
    for load in loads:
        load.start()

    loads[0].wait()
    square = jnp.sum(weight_ref[...] * weight_ref[...], axis=0, keepdims=True)
    for h in range(2):
        for k in range(8):
            lane = h * half + k * part
            ss_own[h, k:k + 1, :] = square[:, lane:lane + part]
    ss_a[0] = ss_own[core]
    def quarter_of(h, p):
        return pl.ds(pl.multiple_of(h * half + p * quarter, quarter), quarter)

    raw[0, x, core] = weight_ref[:, quarter_of(core, 0)]
    raw[1, y, core] = weight_ref[:, quarter_of(core, 1)]

    loads[1].wait()
    loads[2].wait()
    rows = patches_ref[...].astype(F32)
    norm = lax.rsqrt(jnp.sum(rows * rows, axis=1, keepdims=True) + EPS)
    own = pl.ds(pl.multiple_of(z * block, block), block)
    gathered[own, :] = (rows * norm).astype(BF16)

    pl.semaphore_wait(barrier, len(partners))

    for d in far_first(2 * side):
        push(ss_own.at[flip[d % 2]], ss_a.at[d], ss_send.at[0], ss_recv.at[0], at_q[d])

    reach = (depth // 2, depth - 1 - depth // 2)

    def ring_slot(way, d):
        owner = wrap(z + (depth - d if way == 0 else d), depth)
        return gathered.at[pl.ds(pl.multiple_of(owner * block, block), block)]

    def ring_push(way, d, hops):
        slot = ring_slot(way, d)
        push(slot, slot, ring_send.at[way, d + hops], ring_recv.at[way, d + hops],
             at_z[hops if way == 0 else depth - hops])

    def ring_step(s):
        for way in range(2):
            if s == 0:
                ring_push(way, 0, 2)
                ring_push(way, 0, 1)
        for d in (2 * s - 1, 2 * s):
            for way in range(2):
                if 1 <= d <= reach[way]:
                    arrived(ring_slot(way, d), ring_recv.at[way, d])
                    if d + 2 <= reach[way]:
                        ring_push(way, d, 2)

    ring_steps = depth // 4

    ring_step(0)

    moves = []
    for d in far_first(2 * side):
        moves.append(push(weight_ref.at[:, quarter_of(flip[d % 2], 0)], raw.at[0, x, core],
                          raw_send.at[0, d], raw_recv.at[0, d], at_q[d]))
        moves.append(push(weight_ref.at[:, quarter_of(flip[d % 2], 1)], raw.at[1, y, core],
                          raw_send.at[1, d], raw_recv.at[1, d], at_qy[d]))

    for j in range(tokens // 128):
        local = (index_ref[j:j + 1, :] - t * (block * depth)).astype(F32)
        column = jnp.broadcast_to(local, (128, 128)).T
        for k in range(block * depth // 128):
            lane = lax.broadcasted_iota(jnp.int32, (128, 128), 1).astype(F32) + 128 * k
            onehot[128 * j:128 * (j + 1), 128 * k:128 * (k + 1)] = jnp.where(
                column == lane, 1.0, 0.0).astype(BF16)

    ring_step(1)
    settle(ss_a, 2 * side, ss_recv.at[0])
    ss_y[0] = jnp.sum(ss_a[...], axis=0)
    exchange(ss_y, side, at_y, ss_send.at[1], ss_recv.at[1])
    ring_step(2)
    for d in range(1, 2 * side):
        px = wrap(q - d + 2 * side, 2 * side) // 2
        py = wrap(y * 2 + core - d + 2 * side, 2 * side) // 2
        arrived(raw.at[0, px, flip[d % 2]], raw_recv.at[0, d])
        arrived(raw.at[1, py, flip[d % 2]], raw_recv.at[1, d])
    settle(ss_y, side, ss_recv.at[1])
    inverse = lax.rsqrt(jnp.sum(ss_y[...], axis=0) + EPS)
    for k in range(8):
        p, c, lane = k // 4, (k // 2) % 2, (k % 2) * part
        value = raw[p, :, :, :, (k % 4) * part:(k % 4 + 1) * part].reshape(-1, part)
        value = (value * inverse[k:k + 1, :]).astype(BF16).reshape(side, -1, part)
        if p == 0:
            normed[core, 0, c, y, :, :, lane:lane + part] = value
        else:
            normed[core, 1, c, :, x, :, lane:lane + part] = value

    for c in range(2):
        for d in far_first(side):
            moves.append(push(normed.at[core, 0, c, y], normed.at[core, 0, c, y],
                              n2_send.at[0, c, d], n2_recv.at[0, c, d], at_y[d]))
            moves.append(push(normed.at[core, 1, c, :, x], normed.at[core, 1, c, :, x],
                              n2_send.at[1, c, d], n2_recv.at[1, c, d], at_x[d]))
    for s in range(3, ring_steps + 1):
        ring_step(s)
    features[...] = jnp.dot(onehot[...], gathered[...],
                            preferred_element_type=F32).astype(BF16)

    factor = math.log2(math.e) / TEMP
    step_lanes = min(256, group)

    def fill(which, c):
        def chunk(i, carry):
            p = i // (group // step_lanes)
            start = pl.multiple_of(lax.rem(i, group // step_lanes) * step_lanes, step_lanes)
            lanes = pl.ds(start, step_lanes)
            weights = normed[which, p, c, :, :, :, lanes].reshape(width, step_lanes)
            row = which * 4 + p * 2 + c
            target = pl.ds(pl.multiple_of(row * group + start, step_lanes), step_lanes)
            scores = jnp.dot(features[...], weights, preferred_element_type=F32)
            value = jnp.exp2(scores * factor)
            expo[:, target] = value
            total = jnp.sum(value.reshape(tokens // 8, 8, step_lanes), axis=0)
            col_a[0, which, 0, pl.ds(p * 2 + c, 1), lanes] = jnp.sum(total, axis=0, keepdims=True)
            return carry

        lax.fori_loop(0, 2 * (group // step_lanes), chunk, 0)

    def pick(h, first, second):
        return tuple(u * (1 - h) + v * h for u, v in zip(first, second))

    def column_push(it, h):
        for d in far_first(2 * side):
            push(col_a.at[it, h, 0], col_a.at[it, h, d], a_send.at[it, h], a_recv.at[it, h],
                 pick(h, at_q[d], at_qy[d]))

    for c in range(2):
        for d in range(1, side):
            px, py = wrap(x - d + side, side), wrap(y - d + side, side)
            arrived(normed.at[core, 0, c, py], n2_recv.at[0, c, d])
            arrived(normed.at[core, 1, c, :, px], n2_recv.at[1, c, d])
        moves.append(push(normed.at[core, :, c], normed.at[core, :, c],
                           share_send.at[c], share_recv.at[c], sibling))
        fill(core, c)
    column_push(0, core)
    for c in range(2):
        arrived(normed.at[1 - core, :, c], share_recv.at[c])
        fill(1 - core, c)
    column_push(0, 1 - core)

    def row_pass(h):
        def some(g, carry):
            here = pl.ds(pl.multiple_of(g * 64, 64), 64)
            total = jnp.zeros((64, 128), F32) if h == 0 else row_acc[here, :]
            for j in range(half // 128):
                k, l = j // (group // 128), j % (group // 128)
                scale = col_scale[h, k:k + 1, 128 * l:128 * (l + 1)]
                lane = h * half + 128 * j
                total += expo[here, lane:lane + 128] * scale
            row_acc[here, :] = total
            return carry

        lax.fori_loop(0, tokens // 64, some, 0)

    def columns_to_rows(it):
        for h in range(2):
            settle(col_a.at[it, h], 2 * side, a_recv.at[it, h])
            col_b[it, h, 0] = jnp.sum(col_a[it, h], axis=0)
            exchange(col_b.at[it, h], side, (at_y, at_x)[h], b_send.at[it, h], b_recv.at[it, h])
        for h in range(2):
            settle(col_b.at[it, h], side, b_recv.at[it, h])
            col_scale[h] = 1.0 / jnp.sum(col_b[it, h], axis=0)
            row_pass(h)
        for j in range(tokens // 128):
            turned = row_acc[128 * j:128 * (j + 1), :].T
            row_x[it, 0, j:j + 1, :] = jnp.sum(turned, axis=0, keepdims=True)
        exchange(row_x.at[it], depth, at_z, r_send.at[it], r_recv.at[it])

    def rows_to_scale(it):
        settle(row_x.at[it], depth, r_recv.at[it])
        scale = 1.0 / jnp.sum(row_x[it], axis=0)
        for j in range(tokens // 128):
            row_bcast[128 * j:128 * (j + 1), :] = jnp.broadcast_to(
                scale[j:j + 1, :], (128, 128)).T

    def column_pass(it, h):
        def chunk(k, carry):
            target = pl.ds(pl.multiple_of(h * half + k * group, group), group)
            total = jnp.zeros((8, group), F32)
            for g in range(tokens // 64):
                here = slice(g * 64, (g + 1) * 64)
                scale = jnp.concatenate([row_bcast[here, :]] * (group // 128), axis=1)
                value = expo[here, target] * scale
                total += jnp.sum(value.reshape(8, 8, group), axis=0)
            col_a[it, h, 0, pl.ds(k, 1), :] = jnp.sum(total, axis=0, keepdims=True)
            return carry

        lax.fori_loop(0, 4, chunk, 0)

    def sinkhorn(it, carry):
        columns_to_rows(it)
        rows_to_scale(it)
        for h in range(2):
            column_pass(it + 1, h)
            column_push(it + 1, h)
        return carry

    lax.fori_loop(0, ITERS - 1, sinkhorn, 0)
    columns_to_rows(ITERS - 1)

    for way in range(2):
        for d in range(1, reach[way] + 1):
            arrived(ring_slot(way, d), ring_send.at[way, d])
    for copy in moves:
        copy.wait_send()
    settle(ss_a, 2 * side, ss_send.at[0])
    settle(ss_y, side, ss_send.at[1])
    for it in range(ITERS):
        for h in range(2):
            settle(col_a.at[it, h], 2 * side, a_send.at[it, h])
            settle(col_b.at[it, h], side, b_send.at[it, h])
        settle(row_x.at[it], depth, r_send.at[it])

    rows_to_scale(ITERS - 1)


def finish_kernel(scale_out, expo, row_bcast, col_scale, out_ref, staged, sems):
    tokens, columns = expo.shape
    group = columns // 8
    step = staged.shape[1]
    copies = []
    for g in range(tokens // step):
        here = slice(g * step, (g + 1) * step)
        scale = jnp.concatenate([row_bcast[here, :]] * (group // 128), axis=1)
        for k in range(8):
            target = slice(k * group, (k + 1) * group)
            value = scale_out * (expo[here, target] * scale)
            staged[g, :, target] = (value * col_scale[k // 4, k % 4:k % 4 + 1, :]).astype(BF16)
        copies.append(pltpu.make_async_copy(staged.at[g], out_ref.at[pl.ds(g * step, step)],
                                            sems.at[g]))
        copies[-1].start()
    for copy in copies:
        copy.wait()


def body(side, depth, patches, mask_index, proto_weight):
    block, width = patches.shape
    tokens = mask_index.shape[0]
    rows, columns = proto_weight.shape
    half, group = columns // 2, columns // 8
    dma = pltpu.SemaphoreType.DMA
    vmem = pl.BlockSpec(memory_space=pltpu.VMEM)
    hbm = pl.BlockSpec(memory_space=pltpu.HBM)
    expo, row_bcast, col_scale = pl.pallas_call(
        functools.partial(kernel, side, depth),
        out_shape=(
            jax.ShapeDtypeStruct((tokens, columns), F32),
            jax.ShapeDtypeStruct((tokens, 128), F32),
            jax.ShapeDtypeStruct((2, 4, group), F32),
        ),
        in_specs=[hbm] * 3,
        out_specs=(vmem,) * 3,
        scratch_shapes=[
            pltpu.VMEM((block, width), BF16),
            pltpu.VMEM((tokens // 128, 128), jnp.int32),
            pltpu.VMEM((rows, columns), F32),
            pltpu.VMEM((block * depth, width), BF16),
            pltpu.VMEM((tokens, block * depth), BF16),
            pltpu.VMEM((tokens, width), BF16),
            pltpu.VMEM((2, side, 2, rows, half // 2), F32),
            pltpu.VMEM((2, 8, half // 8), F32),
            pltpu.VMEM((2 * side, 8, half // 8), F32),
            pltpu.VMEM((side, 8, half // 8), F32),
            pltpu.VMEM((2, 2, 2, side, side, 2 * rows, group), BF16),
            pltpu.VMEM((tokens, 128), F32),
            pltpu.VMEM((ITERS, 2, 2 * side, 4, group), F32),
            pltpu.VMEM((ITERS, 2, side, 4, group), F32),
            pltpu.VMEM((ITERS, depth, tokens // 128, 128), F32),
            dma((3,)),
            dma((2, depth // 2 + 1)), dma((2, depth // 2 + 1)),
            dma((2, 2 * side)), dma((2, 2 * side)),
            dma((2,)), dma((2,)),
            dma((2, 2, side)), dma((2, 2, side)),
            dma((2,)), dma((2,)),
            dma((ITERS, 2)), dma((ITERS, 2)),
            dma((ITERS, 2)), dma((ITERS, 2)),
            dma((ITERS,)), dma((ITERS,)),
        ],
        compiler_params=pltpu.CompilerParams(
            collective_id=0, has_side_effects=True,
            vmem_limit_bytes=32 * 1024 * 1024,
        ),
        cost_estimate=pl.CostEstimate(
            flops=2 * tokens * columns * width, bytes_accessed=4 * tokens * columns,
            transcendentals=tokens * columns),
    )(*(pltpu.with_memory_space_constraint(v, pltpu.HBM) for v in (
        patches, mask_index.reshape(tokens // 128, 128), proto_weight)))
    step = 64
    return pl.pallas_call(
        functools.partial(finish_kernel, float(columns * depth)),
        out_shape=jax.ShapeDtypeStruct((tokens, columns), BF16),
        in_specs=[vmem] * 3,
        out_specs=hbm,
        scratch_shapes=[pltpu.VMEM((tokens // step, step, columns), BF16),
                        dma((tokens // step,))],
        compiler_params=pltpu.CompilerParams(vmem_limit_bytes=16 * 1024 * 1024),
        cost_estimate=pl.CostEstimate(
            flops=3 * tokens * columns, bytes_accessed=6 * tokens * columns, transcendentals=0),
    )(expo, row_bcast, col_scale)


def solution(mesh):
    side = math.isqrt(mesh.shape["tok"] // 2)
    return jax.shard_map(
        functools.partial(body, side, mesh.shape["proto"]),
        mesh=mesh,
        in_specs=(P(("tok", "proto"), None), P("tok"), P("tok", "proto")),
        out_specs=P("tok", "proto"),
        check_vma=False,
    )
```

```python
import functools
import math

import jax
import jax.numpy as jnp
from jax import lax
from jax.experimental import pallas as pl
from jax.experimental.pallas import tpu as pltpu
from jax.sharding import PartitionSpec as P

ITERS = 3
EPS = 1e-06
TEMP = 0.04
MESH = pl.DeviceIdType.MESH
F32 = jnp.float32
BF16 = jnp.bfloat16


def far_first(n):
    return sorted(range(1, n), key=lambda d: -min(d, n - d))


def kernel(
    side, depth,
    patches_hbm, index_hbm, weight_hbm,
    expo, row_bcast, col_scale,
    patches_ref, index_ref, weight_ref,
    gathered, onehot, features, raw, ss_own, ss_a, ss_y, normed,
    row_acc, col_a, col_b, row_x,
    load_sem, ring_send, ring_recv, raw_send, raw_recv, ss_send, ss_recv,
    n2_send, n2_recv, share_send, share_recv,
    a_send, a_recv, b_send, b_recv, r_send, r_recv,
):
    t = lax.axis_index("tok")
    z = lax.axis_index("proto")
    core = lax.rem(t, 2)
    chip = t // 2
    x = lax.rem(chip, side)
    y = chip // side
    q = lax.rem(t, 2 * side)
    sibling = (t + 1 - 2 * core, z)
    tokens, columns = expo.shape
    half = columns // 2
    quarter = half // 2
    group = columns // 8
    part = half // 8
    block, width = patches_ref.shape

    def wrap(value, n):
        return jnp.where(value >= n, value - n, value)

    at_z, at_q, at_qy, at_x, at_y = {}, {}, {}, {}, {}
    flip = (core, 1 - core)
    for d in range(1, depth):
        at_z[d] = (t, wrap(z + d, depth))
    for d in range(1, 2 * side):
        at_q[d] = (y * (2 * side) + wrap(q + d, 2 * side), z)
        at_qy[d] = ((wrap(y * 2 + core + d, 2 * side) - flip[d % 2]) * side
                    + x * 2 + flip[d % 2], z)
    for d in range(1, side):
        at_x[d] = ((y * side + wrap(x + d, side)) * 2 + core, z)
        at_y[d] = (wrap(y + d, side) * (2 * side) + q, z)

    def push(src, dst, send, recv, device):
        copy = pltpu.make_async_remote_copy(
            src_ref=src, dst_ref=dst, send_sem=send, recv_sem=recv,
            device_id=device, device_id_type=MESH,
        )
        copy.start()
        return copy

    def arrived(ref, sem):
        pltpu.make_async_copy(ref, ref, sem).wait()

    def exchange(buf, n, device, send, recv):
        for d in far_first(n):
            push(buf.at[0], buf.at[d], send, recv, device[d])

    def settle(buf, n, recv):
        arrived(buf.at[pl.ds(1, n - 1)], recv)

    loads = [
        pltpu.make_async_copy(src, dst, load_sem.at[i])
        for i, (src, dst) in enumerate((
            (weight_hbm, weight_ref), (patches_hbm, patches_ref), (index_hbm, index_ref)))
    ]
    for load in loads:
        load.start()

    barrier = pltpu.get_barrier_semaphore()
    partners = (
        [at_z[d] for d in (1, 2, depth - 1, depth - 2)]
        + list(at_q.values()) + list(at_qy.values())
    )
    for device in partners:
        pl.semaphore_signal(barrier, inc=1, device_id=device, device_id_type=MESH)

    loads[0].wait()
    square = jnp.sum(weight_ref[...] * weight_ref[...], axis=0, keepdims=True)
    for h in range(2):
        for k in range(8):
            lane = h * half + k * part
            ss_own[h, k:k + 1, :] = square[:, lane:lane + part]
    ss_a[0] = ss_own[core]

    def quarter_of(h, p):
        return pl.ds(pl.multiple_of(h * half + p * quarter, quarter), quarter)

    raw[0, x, core] = weight_ref[:, quarter_of(core, 0)]
    raw[1, y, core] = weight_ref[:, quarter_of(core, 1)]

    loads[1].wait()
    loads[2].wait()
    rows = patches_ref[...].astype(F32)
    norm = lax.rsqrt(jnp.sum(rows * rows, axis=1, keepdims=True) + EPS)
    own = pl.ds(pl.multiple_of(z * block, block), block)
    gathered[own, :] = (rows * norm).astype(BF16)

    pl.semaphore_wait(barrier, len(partners))

    for d in far_first(2 * side):
        push(ss_own.at[flip[d % 2]], ss_a.at[d], ss_send.at[0], ss_recv.at[0], at_q[d])

    reach = (depth // 2, depth - 1 - depth // 2)

    def ring_slot(way, d):
        owner = wrap(z + (depth - d if way == 0 else d), depth)
        return gathered.at[pl.ds(pl.multiple_of(owner * block, block), block)]

    def ring_push(way, d, hops):
        slot = ring_slot(way, d)
        push(slot, slot, ring_send.at[way, d + hops], ring_recv.at[way, d + hops],
             at_z[hops if way == 0 else depth - hops])

    def ring_step(s):
        for way in range(2):
            if s == 0:
                ring_push(way, 0, 2)
                ring_push(way, 0, 1)
        for d in (2 * s - 1, 2 * s):
            for way in range(2):
                if 1 <= d <= reach[way]:
                    arrived(ring_slot(way, d), ring_recv.at[way, d])
                    if d + 2 <= reach[way]:
                        ring_push(way, d, 2)

    ring_steps = depth // 4

    ring_step(0)

    moves = []
    for d in far_first(2 * side):
        moves.append(push(weight_ref.at[:, quarter_of(flip[d % 2], 0)], raw.at[0, x, core],
                          raw_send.at[0, d], raw_recv.at[0, d], at_q[d]))
        moves.append(push(weight_ref.at[:, quarter_of(flip[d % 2], 1)], raw.at[1, y, core],
                          raw_send.at[1, d], raw_recv.at[1, d], at_qy[d]))

    ring_step(1)
    settle(ss_a, 2 * side, ss_recv.at[0])
    ss_y[0] = jnp.sum(ss_a[...], axis=0)
    exchange(ss_y, side, at_y, ss_send.at[1], ss_recv.at[1])
    ring_step(2)
    for d in range(1, 2 * side):
        px = wrap(q - d + 2 * side, 2 * side) // 2
        py = wrap(y * 2 + core - d + 2 * side, 2 * side) // 2
        arrived(raw.at[0, px, flip[d % 2]], raw_recv.at[0, d])
        arrived(raw.at[1, py, flip[d % 2]], raw_recv.at[1, d])
    settle(ss_y, side, ss_recv.at[1])
    inverse = lax.rsqrt(jnp.sum(ss_y[...], axis=0) + EPS)
    for k in range(8):
        p, c, lane = k // 4, (k // 2) % 2, (k % 2) * part
        value = raw[p, :, :, :, (k % 4) * part:(k % 4 + 1) * part].reshape(-1, part)
        value = (value * inverse[k:k + 1, :]).astype(BF16).reshape(side, -1, part)
        if p == 0:
            normed[core, 0, c, y, :, :, lane:lane + part] = value
        else:
            normed[core, 1, c, :, x, :, lane:lane + part] = value

    for c in range(2):
        for d in far_first(side):
            moves.append(push(normed.at[core, 0, c, y], normed.at[core, 0, c, y],
                              n2_send.at[0, c, d], n2_recv.at[0, c, d], at_y[d]))
            moves.append(push(normed.at[core, 1, c, :, x], normed.at[core, 1, c, :, x],
                              n2_send.at[1, c, d], n2_recv.at[1, c, d], at_x[d]))
        if c == 0:
            for s in range(3, ring_steps):
                ring_step(s)

    for j in range(tokens // 128):
        local = (index_ref[j:j + 1, :] - t * (block * depth)).astype(F32)
        column = jnp.broadcast_to(local, (128, 128)).T
        for k in range(block * depth // 128):
            lane = lax.broadcasted_iota(jnp.int32, (128, 128), 1).astype(F32) + 128 * k
            onehot[128 * j:128 * (j + 1), 128 * k:128 * (k + 1)] = jnp.where(
                column == lane, 1.0, 0.0).astype(BF16)

    ring_step(ring_steps)
    features[...] = jnp.dot(onehot[...], gathered[...],
                            preferred_element_type=F32).astype(BF16)

    factor = math.log2(math.e) / TEMP
    step_lanes = min(256, group)

    def fill(which, c):
        def chunk(i, carry):
            p = i // (group // step_lanes)
            start = pl.multiple_of(lax.rem(i, group // step_lanes) * step_lanes, step_lanes)
            lanes = pl.ds(start, step_lanes)
            weights = normed[which, p, c, :, :, :, lanes].reshape(width, step_lanes)
            row = which * 4 + p * 2 + c
            target = pl.ds(pl.multiple_of(row * group + start, step_lanes), step_lanes)
            scores = jnp.dot(features[...], weights, preferred_element_type=F32)
            value = jnp.exp2(scores * factor)
            expo[:, target] = value
            total = jnp.sum(value.reshape(tokens // 8, 8, step_lanes), axis=0)
            col_a[0, which, 0, pl.ds(p * 2 + c, 1), lanes] = jnp.sum(total, axis=0, keepdims=True)
            return carry

        lax.fori_loop(0, 2 * (group // step_lanes), chunk, 0)

    def pick(h, first, second):
        return tuple(u * (1 - h) + v * h for u, v in zip(first, second))

    def column_push(it, h):
        for d in far_first(2 * side):
            push(col_a.at[it, h, 0], col_a.at[it, h, d], a_send.at[it, h], a_recv.at[it, h],
                 pick(h, at_q[d], at_qy[d]))

    for c in range(2):
        for d in range(1, side):
            px, py = wrap(x - d + side, side), wrap(y - d + side, side)
            arrived(normed.at[core, 0, c, py], n2_recv.at[0, c, d])
            arrived(normed.at[core, 1, c, :, px], n2_recv.at[1, c, d])
        moves.append(push(normed.at[core, :, c], normed.at[core, :, c],
                           share_send.at[c], share_recv.at[c], sibling))
        fill(core, c)
        if c == 1:
            column_push(0, core)
        arrived(normed.at[1 - core, :, c], share_recv.at[c])
        fill(1 - core, c)
    column_push(0, 1 - core)

    def row_pass(h):
        def some(g, carry):
            here = pl.ds(pl.multiple_of(g * 64, 64), 64)
            total = jnp.zeros((64, 128), F32) if h == 0 else row_acc[here, :]
            for j in range(half // 128):
                k, l = j // (group // 128), j % (group // 128)
                scale = col_scale[h, k:k + 1, 128 * l:128 * (l + 1)]
                lane = h * half + 128 * j
                total += expo[here, lane:lane + 128] * scale
            row_acc[here, :] = total
            return carry

        lax.fori_loop(0, tokens // 64, some, 0)

    def columns_to_rows(it):
        for h in range(2):
            settle(col_a.at[it, h], 2 * side, a_recv.at[it, h])
            col_b[it, h, 0] = jnp.sum(col_a[it, h], axis=0)
            exchange(col_b.at[it, h], side, (at_y, at_x)[h], b_send.at[it, h], b_recv.at[it, h])
        for h in range(2):
            settle(col_b.at[it, h], side, b_recv.at[it, h])
            col_scale[h] = 1.0 / jnp.sum(col_b[it, h], axis=0)
            row_pass(h)
        for j in range(tokens // 128):
            turned = row_acc[128 * j:128 * (j + 1), :].T
            row_x[it, 0, j:j + 1, :] = jnp.sum(turned, axis=0, keepdims=True)
        exchange(row_x.at[it], depth, at_z, r_send.at[it], r_recv.at[it])

    def rows_to_scale(it):
        settle(row_x.at[it], depth, r_recv.at[it])
        scale = 1.0 / jnp.sum(row_x[it], axis=0)
        for j in range(tokens // 128):
            row_bcast[128 * j:128 * (j + 1), :] = jnp.broadcast_to(
                scale[j:j + 1, :], (128, 128)).T

    def column_pass(it, h):
        def chunk(k, carry):
            target = pl.ds(pl.multiple_of(h * half + k * group, group), group)
            total = jnp.zeros((8, group), F32)
            for g in range(tokens // 64):
                here = slice(g * 64, (g + 1) * 64)
                scale = jnp.concatenate([row_bcast[here, :]] * (group // 128), axis=1)
                value = expo[here, target] * scale
                total += jnp.sum(value.reshape(8, 8, group), axis=0)
            col_a[it, h, 0, pl.ds(k, 1), :] = jnp.sum(total, axis=0, keepdims=True)
            return carry

        lax.fori_loop(0, 4, chunk, 0)

    def sinkhorn(it, carry):
        columns_to_rows(it)
        rows_to_scale(it)
        for h in range(2):
            column_pass(it + 1, h)
            column_push(it + 1, h)
        return carry

    lax.fori_loop(0, ITERS - 1, sinkhorn, 0)
    columns_to_rows(ITERS - 1)

    for way in range(2):
        for d in range(1, reach[way] + 1):
            arrived(ring_slot(way, d), ring_send.at[way, d])
    for copy in moves:
        copy.wait_send()
    settle(ss_a, 2 * side, ss_send.at[0])
    settle(ss_y, side, ss_send.at[1])
    for it in range(ITERS):
        for h in range(2):
            settle(col_a.at[it, h], 2 * side, a_send.at[it, h])
            settle(col_b.at[it, h], side, b_send.at[it, h])
        settle(row_x.at[it], depth, r_send.at[it])

    rows_to_scale(ITERS - 1)


def finish_kernel(scale_out, expo, row_bcast, col_scale, out_ref, staged, sems):
    tokens, columns = expo.shape
    group = columns // 8
    step = staged.shape[1]
    copies = []
    col = scale_out * col_scale[...]
    for g in range(tokens // step):
        here = slice(g * step, (g + 1) * step)
        scale = jnp.concatenate([row_bcast[here, :]] * (group // 128), axis=1)
        for k in range(8):
            target = slice(k * group, (k + 1) * group)
            value = (expo[here, target] * scale) * col[k // 4, k % 4:k % 4 + 1, :]
            staged[g, :, target] = value.astype(BF16)
        copies.append(pltpu.make_async_copy(staged.at[g], out_ref.at[pl.ds(g * step, step)],
                                            sems.at[g]))
        copies[-1].start()
    for copy in copies:
        copy.wait()


def body(side, depth, patches, mask_index, proto_weight):
    block, width = patches.shape
    tokens = mask_index.shape[0]
    rows, columns = proto_weight.shape
    half, group = columns // 2, columns // 8
    dma = pltpu.SemaphoreType.DMA
    vmem = pl.BlockSpec(memory_space=pltpu.VMEM)
    hbm = pl.BlockSpec(memory_space=pltpu.HBM)
    expo, row_bcast, col_scale = pl.pallas_call(
        functools.partial(kernel, side, depth),
        out_shape=(
            jax.ShapeDtypeStruct((tokens, columns), F32),
            jax.ShapeDtypeStruct((tokens, 128), F32),
            jax.ShapeDtypeStruct((2, 4, group), F32),
        ),
        in_specs=[hbm] * 3,
        out_specs=(vmem,) * 3,
        scratch_shapes=[
            pltpu.VMEM((block, width), BF16),
            pltpu.VMEM((tokens // 128, 128), jnp.int32),
            pltpu.VMEM((rows, columns), F32),
            pltpu.VMEM((block * depth, width), BF16),
            pltpu.VMEM((tokens, block * depth), BF16),
            pltpu.VMEM((tokens, width), BF16),
            pltpu.VMEM((2, side, 2, rows, half // 2), F32),
            pltpu.VMEM((2, 8, half // 8), F32),
            pltpu.VMEM((2 * side, 8, half // 8), F32),
            pltpu.VMEM((side, 8, half // 8), F32),
            pltpu.VMEM((2, 2, 2, side, side, 2 * rows, group), BF16),
            pltpu.VMEM((tokens, 128), F32),
            pltpu.VMEM((ITERS, 2, 2 * side, 4, group), F32),
            pltpu.VMEM((ITERS, 2, side, 4, group), F32),
            pltpu.VMEM((ITERS, depth, tokens // 128, 128), F32),
            dma((3,)),
            dma((2, depth // 2 + 1)), dma((2, depth // 2 + 1)),
            dma((2, 2 * side)), dma((2, 2 * side)),
            dma((2,)), dma((2,)),
            dma((2, 2, side)), dma((2, 2, side)),
            dma((2,)), dma((2,)),
            dma((ITERS, 2)), dma((ITERS, 2)),
            dma((ITERS, 2)), dma((ITERS, 2)),
            dma((ITERS,)), dma((ITERS,)),
        ],
        compiler_params=pltpu.CompilerParams(
            collective_id=0, has_side_effects=True,
            vmem_limit_bytes=32 * 1024 * 1024,
        ),
        cost_estimate=pl.CostEstimate(
            flops=2 * tokens * columns * width, bytes_accessed=4 * tokens * columns,
            transcendentals=tokens * columns),
    )(*(pltpu.with_memory_space_constraint(v, pltpu.HBM) for v in (
        patches, mask_index.reshape(tokens // 128, 128), proto_weight)))
    step = 64
    return pl.pallas_call(
        functools.partial(finish_kernel, float(columns * depth)),
        out_shape=jax.ShapeDtypeStruct((tokens, columns), BF16),
        in_specs=[vmem] * 3,
        out_specs=hbm,
        scratch_shapes=[pltpu.VMEM((tokens // step, step, columns), BF16),
                        dma((tokens // step,))],
        compiler_params=pltpu.CompilerParams(vmem_limit_bytes=16 * 1024 * 1024),
        cost_estimate=pl.CostEstimate(
            flops=3 * tokens * columns, bytes_accessed=6 * tokens * columns, transcendentals=0),
    )(expo, row_bcast, col_scale)


def solution(mesh):
    side = math.isqrt(mesh.shape["tok"] // 2)
    return jax.shard_map(
        functools.partial(body, side, mesh.shape["proto"]),
        mesh=mesh,
        in_specs=(P(("tok", "proto"), None), P("tok"), P("tok", "proto")),
        out_specs=P("tok", "proto"),
        check_vma=False,
    )
```

```python
import functools
import math

import jax
import jax.numpy as jnp
from jax import lax
from jax.experimental import pallas as pl
from jax.experimental.pallas import tpu as pltpu
from jax.sharding import PartitionSpec as P

ITERS = 3
EPS = 1e-06
TEMP = 0.04
MESH = pl.DeviceIdType.MESH
F32 = jnp.float32
BF16 = jnp.bfloat16


def far_first(n):
    return sorted(range(1, n), key=lambda d: -min(d, n - d))


def kernel(
    side, depth,
    patches_hbm, index_hbm, weight_hbm,
    expo, row_bcast, col_scale,
    patches_ref, index_ref, weight_ref,
    gathered, onehot, features, raw, ss_own, ss_a, ss_y, normed,
    row_acc, col_own, col_x, row_x,
    load_sem, ring_send, ring_recv, raw_send, raw_recv, ss_send, ss_recv,
    n2_send, n2_recv, share_send, share_recv,
    a_send, a_recv, r_send, r_recv,
):
    t = lax.axis_index("tok")
    z = lax.axis_index("proto")
    core = lax.rem(t, 2)
    chip = t // 2
    x = lax.rem(chip, side)
    y = chip // side
    q = lax.rem(t, 2 * side)
    sibling = (t + 1 - 2 * core, z)
    tokens, columns = expo.shape
    half = columns // 2
    quarter = half // 2
    group = columns // 8
    part = half // 8
    step_lanes = columns // 16
    plane = 2 * side * side
    block, width = patches_ref.shape

    def wrap(value, n):
        return jnp.where(value >= n, value - n, value)

    at_z, at_q, at_qy, at_x, at_y = {}, {}, {}, {}, {}
    flip = (core, 1 - core)
    for d in range(1, depth):
        at_z[d] = (t, wrap(z + d, depth))
    for d in range(1, 2 * side):
        at_q[d] = (y * (2 * side) + wrap(q + d, 2 * side), z)
        at_qy[d] = ((wrap(y * 2 + core + d, 2 * side) - flip[d % 2]) * side
                    + x * 2 + flip[d % 2], z)
    for d in range(1, side):
        at_x[d] = ((y * side + wrap(x + d, side)) * 2 + core, z)
        at_y[d] = (wrap(y + d, side) * (2 * side) + q, z)

    at_plane = sorted(
        ((min(dy, side - dy) + min(dq, 2 * side - dq) / 2, dy * 2 * side + dq,
          (wrap(y + dy, side) * (2 * side) + wrap(q + dq, 2 * side), z))
         for dy in range(side) for dq in range(2 * side) if dy + dq),
        key=lambda item: (-item[0], item[1]))

    def push(src, dst, send, recv, device):
        copy = pltpu.make_async_remote_copy(
            src_ref=src, dst_ref=dst, send_sem=send, recv_sem=recv,
            device_id=device, device_id_type=MESH,
        )
        copy.start()
        return copy

    def arrived(ref, sem):
        pltpu.make_async_copy(ref, ref, sem).wait()

    def exchange(buf, n, device, send, recv):
        for d in far_first(n):
            push(buf.at[0], buf.at[d], send, recv, device[d])

    def settle(buf, n, recv):
        arrived(buf.at[pl.ds(1, n - 1)], recv)

    loads = [
        pltpu.make_async_copy(src, dst, load_sem.at[i])
        for i, (src, dst) in enumerate((
            (weight_hbm, weight_ref), (patches_hbm, patches_ref), (index_hbm, index_ref)))
    ]
    for load in loads:
        load.start()

    barrier = pltpu.get_barrier_semaphore()
    partners = (
        [at_z[d] for d in (1, 2, depth - 1, depth - 2)]
        + list(at_q.values()) + list(at_qy.values())
    )
    for device in partners:
        pl.semaphore_signal(barrier, inc=1, device_id=device, device_id_type=MESH)

    loads[0].wait()
    square = jnp.sum(weight_ref[...] * weight_ref[...], axis=0, keepdims=True)
    for h in range(2):
        for k in range(8):
            lane = h * half + k * part
            ss_own[h, k:k + 1, :] = square[:, lane:lane + part]
    ss_a[0] = ss_own[core]

    def quarter_of(h, p):
        return pl.ds(pl.multiple_of(h * half + p * quarter, quarter), quarter)

    raw[0, x, core] = weight_ref[:, quarter_of(core, 0)]
    raw[1, y, core] = weight_ref[:, quarter_of(core, 1)]

    loads[1].wait()
    loads[2].wait()
    rows = patches_ref[...].astype(F32)
    norm = lax.rsqrt(jnp.sum(rows * rows, axis=1, keepdims=True) + EPS)
    own = pl.ds(pl.multiple_of(z * block, block), block)
    gathered[own, :] = (rows * norm).astype(BF16)

    pl.semaphore_wait(barrier, len(partners))

    for d in far_first(2 * side):
        push(ss_own.at[flip[d % 2]], ss_a.at[d], ss_send.at[0], ss_recv.at[0], at_q[d])

    reach = (depth // 2, depth - 1 - depth // 2)

    def ring_slot(way, d):
        owner = wrap(z + (depth - d if way == 0 else d), depth)
        return gathered.at[pl.ds(pl.multiple_of(owner * block, block), block)]

    def ring_push(way, d, hops):
        slot = ring_slot(way, d)
        push(slot, slot, ring_send.at[way, d + hops], ring_recv.at[way, d + hops],
             at_z[hops if way == 0 else depth - hops])

    def ring_step(s):
        for way in range(2):
            if s == 0:
                ring_push(way, 0, 2)
                ring_push(way, 0, 1)
        for d in (2 * s - 1, 2 * s):
            for way in range(2):
                if 1 <= d <= reach[way]:
                    arrived(ring_slot(way, d), ring_recv.at[way, d])
                    if d + 2 <= reach[way]:
                        ring_push(way, d, 2)

    ring_steps = depth // 4

    ring_step(0)

    moves = []
    for d in far_first(2 * side):
        moves.append(push(weight_ref.at[:, quarter_of(flip[d % 2], 0)], raw.at[0, x, core],
                          raw_send.at[0, d], raw_recv.at[0, d], at_q[d]))
        moves.append(push(weight_ref.at[:, quarter_of(flip[d % 2], 1)], raw.at[1, y, core],
                          raw_send.at[1, d], raw_recv.at[1, d], at_qy[d]))

    ring_step(1)
    settle(ss_a, 2 * side, ss_recv.at[0])
    ss_y[0] = jnp.sum(ss_a[...], axis=0)
    exchange(ss_y, side, at_y, ss_send.at[1], ss_recv.at[1])
    ring_step(2)
    for d in range(1, 2 * side):
        px = wrap(q - d + 2 * side, 2 * side) // 2
        py = wrap(y * 2 + core - d + 2 * side, 2 * side) // 2
        arrived(raw.at[0, px, flip[d % 2]], raw_recv.at[0, d])
        arrived(raw.at[1, py, flip[d % 2]], raw_recv.at[1, d])
    settle(ss_y, side, ss_recv.at[1])
    inverse = lax.rsqrt(jnp.sum(ss_y[...], axis=0) + EPS)
    for k in range(8):
        p, c, lane = k // 4, (k // 2) % 2, (k % 2) * part
        value = raw[p, :, :, :, (k % 4) * part:(k % 4 + 1) * part].reshape(-1, part)
        value = (value * inverse[k:k + 1, :]).astype(BF16).reshape(side, -1, part)
        if p == 0:
            normed[core, 0, c, y, :, :, lane:lane + part] = value
        else:
            normed[core, 1, c, :, x, :, lane:lane + part] = value

    for c in range(2):
        for d in far_first(side):
            moves.append(push(normed.at[core, 0, c, y], normed.at[core, 0, c, y],
                              n2_send.at[0, c, d], n2_recv.at[0, c, d], at_y[d]))
            moves.append(push(normed.at[core, 1, c, :, x], normed.at[core, 1, c, :, x],
                              n2_send.at[1, c, d], n2_recv.at[1, c, d], at_x[d]))
        if c == 0:
            for s in range(3, ring_steps):
                ring_step(s)

    for j in range(tokens // 128):
        local = (index_ref[j:j + 1, :] - t * (block * depth)).astype(F32)
        column = jnp.broadcast_to(local, (128, 128)).T
        for k in range(block * depth // 128):
            lane = lax.broadcasted_iota(jnp.int32, (128, 128), 1).astype(F32) + 128 * k
            onehot[128 * j:128 * (j + 1), 128 * k:128 * (k + 1)] = jnp.where(
                column == lane, 1.0, 0.0).astype(BF16)

    ring_step(ring_steps)
    features[...] = jnp.dot(onehot[...], gathered[...],
                            preferred_element_type=F32).astype(BF16)

    factor = math.log2(math.e) / TEMP

    def fill(which, c):
        def chunk(i, carry):
            p = i // (group // step_lanes)
            start = pl.multiple_of(lax.rem(i, group // step_lanes) * step_lanes, step_lanes)
            lanes = pl.ds(start, step_lanes)
            weights = normed[which, p, c, :, :, :, lanes].reshape(width, step_lanes)
            row = (which * 4 + p * 2 + c) * (group // step_lanes) + start // step_lanes
            target = pl.ds(pl.multiple_of(row * step_lanes, step_lanes), step_lanes)
            scores = jnp.dot(features[...], weights, preferred_element_type=F32)
            value = jnp.exp2(scores * factor)
            expo[:, target] = value
            total = jnp.sum(value.reshape(tokens // 8, 8, step_lanes), axis=0)
            col_own[pl.ds(row, 1), :] = jnp.sum(total, axis=0, keepdims=True)
            return carry

        lax.fori_loop(0, 2 * (group // step_lanes), chunk, 0)

    def column_push(it):
        col_x[it, 0] = col_own[...].astype(BF16)
        for _, slot, device in at_plane:
            push(col_x.at[it, 0], col_x.at[it, slot], a_send.at[it], a_recv.at[it], device)

    for c in range(2):
        for d in range(1, side):
            px, py = wrap(x - d + side, side), wrap(y - d + side, side)
            arrived(normed.at[core, 0, c, py], n2_recv.at[0, c, d])
            arrived(normed.at[core, 1, c, :, px], n2_recv.at[1, c, d])
        moves.append(push(normed.at[core, :, c], normed.at[core, :, c],
                          share_send.at[c], share_recv.at[c], sibling))
        fill(core, c)
    for c in range(2):
        arrived(normed.at[1 - core, :, c], share_recv.at[c])
        fill(1 - core, c)
    column_push(0)

    def columns_to_rows(it):
        settle(col_x.at[it], plane, a_recv.at[it])
        col_scale[...] = 1.0 / jnp.sum(col_x[it].astype(F32), axis=0)

        def some(g, carry):
            here = pl.ds(pl.multiple_of(g * 64, 64), 64)
            total = jnp.zeros((64, 128), F32)
            for j in range(columns // 128):
                k, l = j // (step_lanes // 128), j % (step_lanes // 128)
                scale = col_scale[k:k + 1, 128 * l:128 * (l + 1)]
                total += expo[here, 128 * j:128 * (j + 1)] * scale
            row_acc[here, :] = total
            return carry

        lax.fori_loop(0, tokens // 64, some, 0)
        for j in range(tokens // 128):
            turned = row_acc[128 * j:128 * (j + 1), :].T
            row_x[it, 0, j:j + 1, :] = jnp.sum(turned, axis=0, keepdims=True)
        exchange(row_x.at[it], depth, at_z, r_send.at[it], r_recv.at[it])

    def rows_to_scale(it):
        settle(row_x.at[it], depth, r_recv.at[it])
        scale = 1.0 / jnp.sum(row_x[it], axis=0)
        for j in range(tokens // 128):
            row_bcast[128 * j:128 * (j + 1), :] = jnp.broadcast_to(
                scale[j:j + 1, :], (128, 128)).T

    def column_pass():
        def chunk(k, carry):
            target = pl.ds(pl.multiple_of(k * group, group), group)
            total = jnp.zeros((8, group), F32)
            for g in range(tokens // 64):
                here = slice(g * 64, (g + 1) * 64)
                scale = jnp.concatenate([row_bcast[here, :]] * (group // 128), axis=1)
                value = expo[here, target] * scale
                total += jnp.sum(value.reshape(8, 8, group), axis=0)
            total = jnp.sum(total, axis=0, keepdims=True)
            for i in range(group // step_lanes):
                col_own[pl.ds(k * (group // step_lanes) + i, 1), :] = (
                    total[:, i * step_lanes:(i + 1) * step_lanes])
            return carry

        lax.fori_loop(0, 8, chunk, 0)

    def sinkhorn(it, carry):
        columns_to_rows(it)
        rows_to_scale(it)
        column_pass()
        column_push(it + 1)
        return carry

    lax.fori_loop(0, ITERS - 1, sinkhorn, 0)
    columns_to_rows(ITERS - 1)

    for way in range(2):
        for d in range(1, reach[way] + 1):
            arrived(ring_slot(way, d), ring_send.at[way, d])
    for copy in moves:
        copy.wait_send()
    settle(ss_a, 2 * side, ss_send.at[0])
    settle(ss_y, side, ss_send.at[1])
    for it in range(ITERS):
        settle(col_x.at[it], plane, a_send.at[it])
        settle(row_x.at[it], depth, r_send.at[it])

    rows_to_scale(ITERS - 1)


def finish_kernel(scale_out, expo, row_bcast, col_scale, out_ref, staged, sems):
    tokens, columns = expo.shape
    group = columns // 16
    step = staged.shape[1]
    copies = []
    col = scale_out * col_scale[...]
    for g in range(tokens // step):
        here = slice(g * step, (g + 1) * step)
        scale = jnp.concatenate([row_bcast[here, :]] * (group // 128), axis=1)
        for k in range(16):
            target = slice(k * group, (k + 1) * group)
            value = (expo[here, target] * scale) * col[k:k + 1, :]
            staged[g, :, target] = value.astype(BF16)
        copies.append(pltpu.make_async_copy(staged.at[g], out_ref.at[pl.ds(g * step, step)],
                                            sems.at[g]))
        copies[-1].start()
    for copy in copies:
        copy.wait()


def body(side, depth, patches, mask_index, proto_weight):
    block, width = patches.shape
    tokens = mask_index.shape[0]
    rows, columns = proto_weight.shape
    half, group = columns // 2, columns // 8
    dma = pltpu.SemaphoreType.DMA
    vmem = pl.BlockSpec(memory_space=pltpu.VMEM)
    hbm = pl.BlockSpec(memory_space=pltpu.HBM)
    expo, row_bcast, col_scale = pl.pallas_call(
        functools.partial(kernel, side, depth),
        out_shape=(
            jax.ShapeDtypeStruct((tokens, columns), F32),
            jax.ShapeDtypeStruct((tokens, 128), F32),
            jax.ShapeDtypeStruct((16, columns // 16), F32),
        ),
        in_specs=[hbm] * 3,
        out_specs=(vmem,) * 3,
        scratch_shapes=[
            pltpu.VMEM((block, width), BF16),
            pltpu.VMEM((tokens // 128, 128), jnp.int32),
            pltpu.VMEM((rows, columns), F32),
            pltpu.VMEM((block * depth, width), BF16),
            pltpu.VMEM((tokens, block * depth), BF16),
            pltpu.VMEM((tokens, width), BF16),
            pltpu.VMEM((2, side, 2, rows, half // 2), F32),
            pltpu.VMEM((2, 8, half // 8), F32),
            pltpu.VMEM((2 * side, 8, half // 8), F32),
            pltpu.VMEM((side, 8, half // 8), F32),
            pltpu.VMEM((2, 2, 2, side, side, 2 * rows, group), BF16),
            pltpu.VMEM((tokens, 128), F32),
            pltpu.VMEM((16, columns // 16), F32),
            pltpu.VMEM((ITERS, 2 * side * side, 16, columns // 16), BF16),
            pltpu.VMEM((ITERS, depth, tokens // 128, 128), F32),
            dma((3,)),
            dma((2, depth // 2 + 1)), dma((2, depth // 2 + 1)),
            dma((2, 2 * side)), dma((2, 2 * side)),
            dma((2,)), dma((2,)),
            dma((2, 2, side)), dma((2, 2, side)),
            dma((2,)), dma((2,)),
            dma((ITERS,)), dma((ITERS,)),
            dma((ITERS,)), dma((ITERS,)),
        ],
        compiler_params=pltpu.CompilerParams(
            collective_id=0, has_side_effects=True,
            vmem_limit_bytes=32 * 1024 * 1024,
        ),
        cost_estimate=pl.CostEstimate(
            flops=2 * tokens * columns * width, bytes_accessed=4 * tokens * columns,
            transcendentals=tokens * columns),
    )(*(pltpu.with_memory_space_constraint(v, pltpu.HBM) for v in (
        patches, mask_index.reshape(tokens // 128, 128), proto_weight)))
    step = 64
    return pl.pallas_call(
        functools.partial(finish_kernel, float(columns * depth)),
        out_shape=jax.ShapeDtypeStruct((tokens, columns), BF16),
        in_specs=[vmem] * 3,
        out_specs=hbm,
        scratch_shapes=[pltpu.VMEM((tokens // step, step, columns), BF16),
                        dma((tokens // step,))],
        compiler_params=pltpu.CompilerParams(vmem_limit_bytes=16 * 1024 * 1024),
        cost_estimate=pl.CostEstimate(
            flops=3 * tokens * columns, bytes_accessed=6 * tokens * columns, transcendentals=0),
    )(expo, row_bcast, col_scale)


def solution(mesh):
    side = math.isqrt(mesh.shape["tok"] // 2)
    return jax.shard_map(
        functools.partial(body, side, mesh.shape["proto"]),
        mesh=mesh,
        in_specs=(P(("tok", "proto"), None), P("tok"), P("tok", "proto")),
        out_specs=P("tok", "proto"),
        check_vma=False,
    )
```

```python
import functools
import math

import jax
import jax.numpy as jnp
from jax import lax
from jax.experimental import pallas as pl
from jax.experimental.pallas import tpu as pltpu
from jax.sharding import PartitionSpec as P

ITERS = 3
EPS = 1e-06
TEMP = 0.04
MESH = pl.DeviceIdType.MESH
F32 = jnp.float32
BF16 = jnp.bfloat16


def far_first(n):
    return sorted(range(1, n), key=lambda d: -min(d, n - d))


def kernel(
    side, depth,
    patches_hbm, index_hbm, weight_hbm,
    expo, row_bcast,
    patches_ref, index_ref, weight_ref,
    gathered, onehot, features, raw, ss_own, ss_a, ss_y, normed,
    row_acc, col_own, col_scale, col_x, row_x,
    load_sem, ring_send, ring_recv, raw_send, raw_recv, ss_send, ss_recv,
    n2_send, n2_recv, share_send, share_recv,
    a_send, a_recv, r_send, r_recv,
):
    t = lax.axis_index("tok")
    z = lax.axis_index("proto")
    core = lax.rem(t, 2)
    chip = t // 2
    x = lax.rem(chip, side)
    y = chip // side
    q = lax.rem(t, 2 * side)
    sibling = (t + 1 - 2 * core, z)
    tokens, columns = expo.shape
    half = columns // 2
    quarter = half // 2
    group = columns // 8
    part = half // 8
    step_lanes = columns // 16
    plane = 2 * side * side
    block, width = patches_ref.shape

    def wrap(value, n):
        return jnp.where(value >= n, value - n, value)

    at_z, at_q, at_qy, at_x, at_y = {}, {}, {}, {}, {}
    flip = (core, 1 - core)
    for d in range(1, depth):
        at_z[d] = (t, wrap(z + d, depth))
    for d in range(1, 2 * side):
        at_q[d] = (y * (2 * side) + wrap(q + d, 2 * side), z)
        at_qy[d] = ((wrap(y * 2 + core + d, 2 * side) - flip[d % 2]) * side
                    + x * 2 + flip[d % 2], z)
    for d in range(1, side):
        at_x[d] = ((y * side + wrap(x + d, side)) * 2 + core, z)
        at_y[d] = (wrap(y + d, side) * (2 * side) + q, z)

    at_plane = sorted(
        ((min(dy, side - dy) + min(dq, 2 * side - dq) / 2, dy * 2 * side + dq,
          (wrap(y + dy, side) * (2 * side) + wrap(q + dq, 2 * side), z))
         for dy in range(side) for dq in range(2 * side) if dy + dq),
        key=lambda item: (-item[0], item[1]))

    def push(src, dst, send, recv, device):
        copy = pltpu.make_async_remote_copy(
            src_ref=src, dst_ref=dst, send_sem=send, recv_sem=recv,
            device_id=device, device_id_type=MESH,
        )
        copy.start()
        return copy

    def arrived(ref, sem):
        pltpu.make_async_copy(ref, ref, sem).wait()

    def exchange(buf, n, device, send, recv):
        for d in far_first(n):
            push(buf.at[0], buf.at[d], send, recv, device[d])

    def settle(buf, n, recv):
        arrived(buf.at[pl.ds(1, n - 1)], recv)

    loads = [
        pltpu.make_async_copy(src, dst, load_sem.at[i])
        for i, (src, dst) in enumerate((
            (weight_hbm, weight_ref), (patches_hbm, patches_ref), (index_hbm, index_ref)))
    ]
    for load in loads:
        load.start()

    barrier = pltpu.get_barrier_semaphore()
    partners = (
        [at_z[d] for d in (1, 2, depth - 1, depth - 2)]
        + list(at_q.values()) + list(at_qy.values())
    )
    for device in partners:
        pl.semaphore_signal(barrier, inc=1, device_id=device, device_id_type=MESH)

    loads[0].wait()
    square = jnp.sum(weight_ref[...] * weight_ref[...], axis=0, keepdims=True)
    for h in range(2):
        for k in range(8):
            lane = h * half + k * part
            ss_own[h, k:k + 1, :] = square[:, lane:lane + part]
    ss_a[0] = ss_own[core]

    def quarter_of(h, p):
        return pl.ds(pl.multiple_of(h * half + p * quarter, quarter), quarter)

    raw[0, x, core] = weight_ref[:, quarter_of(core, 0)]
    raw[1, y, core] = weight_ref[:, quarter_of(core, 1)]

    loads[1].wait()
    loads[2].wait()
    rows = patches_ref[...].astype(F32)
    norm = lax.rsqrt(jnp.sum(rows * rows, axis=1, keepdims=True) + EPS)
    own = pl.ds(pl.multiple_of(z * block, block), block)
    gathered[own, :] = (rows * norm).astype(BF16)

    pl.semaphore_wait(barrier, len(partners))

    for d in far_first(2 * side):
        push(ss_own.at[flip[d % 2]], ss_a.at[d], ss_send.at[0], ss_recv.at[0], at_q[d])

    reach = (depth // 2, depth - 1 - depth // 2)

    def ring_slot(way, d):
        owner = wrap(z + (depth - d if way == 0 else d), depth)
        return gathered.at[pl.ds(pl.multiple_of(owner * block, block), block)]

    def ring_push(way, d, hops):
        slot = ring_slot(way, d)
        push(slot, slot, ring_send.at[way, d + hops], ring_recv.at[way, d + hops],
             at_z[hops if way == 0 else depth - hops])

    def ring_step(s):
        for way in range(2):
            if s == 0:
                ring_push(way, 0, 2)
                ring_push(way, 0, 1)
        for d in (2 * s - 1, 2 * s):
            for way in range(2):
                if 1 <= d <= reach[way]:
                    arrived(ring_slot(way, d), ring_recv.at[way, d])
                    if d + 2 <= reach[way]:
                        ring_push(way, d, 2)

    ring_steps = depth // 4

    ring_step(0)

    moves = []
    for d in far_first(2 * side):
        moves.append(push(weight_ref.at[:, quarter_of(flip[d % 2], 0)], raw.at[0, x, core],
                          raw_send.at[0, d], raw_recv.at[0, d], at_q[d]))
        moves.append(push(weight_ref.at[:, quarter_of(flip[d % 2], 1)], raw.at[1, y, core],
                          raw_send.at[1, d], raw_recv.at[1, d], at_qy[d]))

    ring_step(1)
    settle(ss_a, 2 * side, ss_recv.at[0])
    ss_y[0] = jnp.sum(ss_a[...], axis=0)
    exchange(ss_y, side, at_y, ss_send.at[1], ss_recv.at[1])
    ring_step(2)
    for d in range(1, 2 * side):
        px = wrap(q - d + 2 * side, 2 * side) // 2
        py = wrap(y * 2 + core - d + 2 * side, 2 * side) // 2
        arrived(raw.at[0, px, flip[d % 2]], raw_recv.at[0, d])
        arrived(raw.at[1, py, flip[d % 2]], raw_recv.at[1, d])
    settle(ss_y, side, ss_recv.at[1])
    inverse = lax.rsqrt(jnp.sum(ss_y[...], axis=0) + EPS)
    for k in range(8):
        p, c, lane = k // 4, (k // 2) % 2, (k % 2) * part
        value = raw[p, :, :, :, (k % 4) * part:(k % 4 + 1) * part].reshape(-1, part)
        value = (value * inverse[k:k + 1, :]).astype(BF16).reshape(side, -1, part)
        if p == 0:
            normed[core, 0, c, y, :, :, lane:lane + part] = value
        else:
            normed[core, 1, c, :, x, :, lane:lane + part] = value

    for c in range(2):
        for d in far_first(side):
            moves.append(push(normed.at[core, 0, c, y], normed.at[core, 0, c, y],
                              n2_send.at[0, c, d], n2_recv.at[0, c, d], at_y[d]))
            moves.append(push(normed.at[core, 1, c, :, x], normed.at[core, 1, c, :, x],
                              n2_send.at[1, c, d], n2_recv.at[1, c, d], at_x[d]))
        if c == 0:
            for s in range(3, ring_steps):
                ring_step(s)

    for j in range(tokens // 128):
        local = (index_ref[j:j + 1, :] - t * (block * depth)).astype(F32)
        column = jnp.broadcast_to(local, (128, 128)).T
        for k in range(block * depth // 128):
            lane = lax.broadcasted_iota(jnp.int32, (128, 128), 1).astype(F32) + 128 * k
            onehot[128 * j:128 * (j + 1), 128 * k:128 * (k + 1)] = jnp.where(
                column == lane, 1.0, 0.0).astype(BF16)

    ring_step(ring_steps)
    features[...] = jnp.dot(onehot[...], gathered[...],
                            preferred_element_type=F32).astype(BF16)

    factor = math.log2(math.e) / TEMP

    def fill(which, c):
        def chunk(i, carry):
            p = i // (group // step_lanes)
            start = pl.multiple_of(lax.rem(i, group // step_lanes) * step_lanes, step_lanes)
            lanes = pl.ds(start, step_lanes)
            weights = normed[which, p, c, :, :, :, lanes].reshape(width, step_lanes)
            row = (which * 4 + p * 2 + c) * (group // step_lanes) + start // step_lanes
            target = pl.ds(pl.multiple_of(row * step_lanes, step_lanes), step_lanes)
            scores = jnp.dot(features[...], weights, preferred_element_type=F32)
            value = jnp.exp2(scores * factor)
            expo[:, target] = value
            total = jnp.sum(value.reshape(tokens // 8, 8, step_lanes), axis=0)
            col_own[pl.ds(row, 1), :] = jnp.sum(total, axis=0, keepdims=True)
            return carry

        lax.fori_loop(0, 2 * (group // step_lanes), chunk, 0)

    def column_push(it):
        col_x[it, 0] = col_own[...].astype(BF16)
        for _, slot, device in at_plane:
            push(col_x.at[it, 0], col_x.at[it, slot], a_send.at[it], a_recv.at[it], device)

    for c in range(2):
        for d in range(1, side):
            px, py = wrap(x - d + side, side), wrap(y - d + side, side)
            arrived(normed.at[core, 0, c, py], n2_recv.at[0, c, d])
            arrived(normed.at[core, 1, c, :, px], n2_recv.at[1, c, d])
        moves.append(push(normed.at[core, :, c], normed.at[core, :, c],
                          share_send.at[c], share_recv.at[c], sibling))
        fill(core, c)
    for c in range(2):
        arrived(normed.at[1 - core, :, c], share_recv.at[c])
        fill(1 - core, c)
    column_push(0)

    def columns_to_rows(it, last=False):
        settle(col_x.at[it], plane, a_recv.at[it])
        col_scale[...] = 1.0 / jnp.sum(col_x[it].astype(F32), axis=0)

        def some(g, carry):
            here = pl.ds(pl.multiple_of(g * 64, 64), 64)
            total = jnp.zeros((64, 128), F32)
            for j in range(columns // 128):
                k, l = j // (step_lanes // 128), j % (step_lanes // 128)
                scale = col_scale[k:k + 1, 128 * l:128 * (l + 1)]
                value = expo[here, 128 * j:128 * (j + 1)] * scale
                total += value
                if last:
                    expo[here, 128 * j:128 * (j + 1)] = value
            row_acc[here, :] = total
            return carry

        lax.fori_loop(0, tokens // 64, some, 0)
        for j in range(tokens // 128):
            turned = row_acc[128 * j:128 * (j + 1), :].T
            row_x[it, 0, j:j + 1, :] = jnp.sum(turned, axis=0, keepdims=True)
        exchange(row_x.at[it], depth, at_z, r_send.at[it], r_recv.at[it])

    def rows_to_scale(it):
        settle(row_x.at[it], depth, r_recv.at[it])
        scale = 1.0 / jnp.sum(row_x[it], axis=0)
        for j in range(tokens // 128):
            row_bcast[128 * j:128 * (j + 1), :] = jnp.broadcast_to(
                scale[j:j + 1, :], (128, 128)).T

    def column_pass():
        def chunk(k, carry):
            target = pl.ds(pl.multiple_of(k * group, group), group)
            total = jnp.zeros((8, group), F32)
            for g in range(tokens // 64):
                here = slice(g * 64, (g + 1) * 64)
                scale = jnp.concatenate([row_bcast[here, :]] * (group // 128), axis=1)
                value = expo[here, target] * scale
                total += jnp.sum(value.reshape(8, 8, group), axis=0)
            total = jnp.sum(total, axis=0, keepdims=True)
            for i in range(group // step_lanes):
                col_own[pl.ds(k * (group // step_lanes) + i, 1), :] = (
                    total[:, i * step_lanes:(i + 1) * step_lanes])
            return carry

        lax.fori_loop(0, 8, chunk, 0)

    def sinkhorn(it, carry):
        columns_to_rows(it)
        rows_to_scale(it)
        column_pass()
        column_push(it + 1)
        return carry

    lax.fori_loop(0, ITERS - 1, sinkhorn, 0)
    columns_to_rows(ITERS - 1, last=True)

    for way in range(2):
        for d in range(1, reach[way] + 1):
            arrived(ring_slot(way, d), ring_send.at[way, d])
    for copy in moves:
        copy.wait_send()
    settle(ss_a, 2 * side, ss_send.at[0])
    settle(ss_y, side, ss_send.at[1])
    for it in range(ITERS):
        settle(col_x.at[it], plane, a_send.at[it])
        settle(row_x.at[it], depth, r_send.at[it])

    rows_to_scale(ITERS - 1)


def finish_kernel(scale_out, expo, row_bcast, out_ref, staged, sems):
    tokens, columns = expo.shape
    group = columns // 8
    step = staged.shape[1]
    copies = []
    for g in range(tokens // step):
        here = slice(g * step, (g + 1) * step)
        scale = jnp.concatenate([scale_out * row_bcast[here, :]] * (group // 128), axis=1)
        for k in range(8):
            target = slice(k * group, (k + 1) * group)
            staged[g, :, target] = (expo[here, target] * scale).astype(BF16)
        copies.append(pltpu.make_async_copy(staged.at[g], out_ref.at[pl.ds(g * step, step)],
                                            sems.at[g]))
        copies[-1].start()
    for copy in copies:
        copy.wait()


def body(side, depth, patches, mask_index, proto_weight):
    block, width = patches.shape
    tokens = mask_index.shape[0]
    rows, columns = proto_weight.shape
    half, group = columns // 2, columns // 8
    dma = pltpu.SemaphoreType.DMA
    vmem = pl.BlockSpec(memory_space=pltpu.VMEM)
    hbm = pl.BlockSpec(memory_space=pltpu.HBM)
    expo, row_bcast = pl.pallas_call(
        functools.partial(kernel, side, depth),
        out_shape=(
            jax.ShapeDtypeStruct((tokens, columns), F32),
            jax.ShapeDtypeStruct((tokens, 128), F32),
        ),
        in_specs=[hbm] * 3,
        out_specs=(vmem,) * 2,
        scratch_shapes=[
            pltpu.VMEM((block, width), BF16),
            pltpu.VMEM((tokens // 128, 128), jnp.int32),
            pltpu.VMEM((rows, columns), F32),
            pltpu.VMEM((block * depth, width), BF16),
            pltpu.VMEM((tokens, block * depth), BF16),
            pltpu.VMEM((tokens, width), BF16),
            pltpu.VMEM((2, side, 2, rows, half // 2), F32),
            pltpu.VMEM((2, 8, half // 8), F32),
            pltpu.VMEM((2 * side, 8, half // 8), F32),
            pltpu.VMEM((side, 8, half // 8), F32),
            pltpu.VMEM((2, 2, 2, side, side, 2 * rows, group), BF16),
            pltpu.VMEM((tokens, 128), F32),
            pltpu.VMEM((16, columns // 16), F32),
            pltpu.VMEM((16, columns // 16), F32),
            pltpu.VMEM((ITERS, 2 * side * side, 16, columns // 16), BF16),
            pltpu.VMEM((ITERS, depth, tokens // 128, 128), F32),
            dma((3,)),
            dma((2, depth // 2 + 1)), dma((2, depth // 2 + 1)),
            dma((2, 2 * side)), dma((2, 2 * side)),
            dma((2,)), dma((2,)),
            dma((2, 2, side)), dma((2, 2, side)),
            dma((2,)), dma((2,)),
            dma((ITERS,)), dma((ITERS,)),
            dma((ITERS,)), dma((ITERS,)),
        ],
        compiler_params=pltpu.CompilerParams(
            collective_id=0, has_side_effects=True,
            vmem_limit_bytes=32 * 1024 * 1024,
        ),
        cost_estimate=pl.CostEstimate(
            flops=2 * tokens * columns * width, bytes_accessed=4 * tokens * columns,
            transcendentals=tokens * columns),
    )(*(pltpu.with_memory_space_constraint(v, pltpu.HBM) for v in (
        patches, mask_index.reshape(tokens // 128, 128), proto_weight)))
    step = 32
    return pl.pallas_call(
        functools.partial(finish_kernel, float(columns * depth)),
        out_shape=jax.ShapeDtypeStruct((tokens, columns), BF16),
        in_specs=[vmem] * 2,
        out_specs=hbm,
        scratch_shapes=[pltpu.VMEM((tokens // step, step, columns), BF16),
                        dma((tokens // step,))],
        compiler_params=pltpu.CompilerParams(vmem_limit_bytes=16 * 1024 * 1024),
        cost_estimate=pl.CostEstimate(
            flops=3 * tokens * columns, bytes_accessed=6 * tokens * columns, transcendentals=0),
    )(expo, row_bcast)


def solution(mesh):
    side = math.isqrt(mesh.shape["tok"] // 2)
    return jax.shard_map(
        functools.partial(body, side, mesh.shape["proto"]),
        mesh=mesh,
        in_specs=(P(("tok", "proto"), None), P("tok"), P("tok", "proto")),
        out_specs=P("tok", "proto"),
        check_vma=False,
    )
```

```python
import functools
import math

import jax
import jax.numpy as jnp
from jax import lax
from jax.experimental import pallas as pl
from jax.experimental.pallas import tpu as pltpu
from jax.sharding import PartitionSpec as P

ITERS = 3
EPS = 1e-06
TEMP = 0.04
MESH = pl.DeviceIdType.MESH
F32 = jnp.float32
BF16 = jnp.bfloat16


def far_first(n):
    return sorted(range(1, n), key=lambda d: -min(d, n - d))


def kernel(
    side, depth,
    patches_hbm, index_hbm, weight_hbm,
    expo, row_bcast,
    patches_ref, index_ref, weight_ref,
    gathered, onehot, features, raw, ss_own, ss_a, ss_y, normed,
    row_acc, col_own, col_scale, col_x, row_x,
    load_sem, ring_send, ring_recv, raw_send, raw_recv, ss_send, ss_recv,
    n2_send, n2_recv, share_send, share_recv,
    a_send, a_recv, r_send, r_recv,
):
    t = lax.axis_index("tok")
    z = lax.axis_index("proto")
    core = lax.rem(t, 2)
    chip = t // 2
    x = lax.rem(chip, side)
    y = chip // side
    q = lax.rem(t, 2 * side)
    sibling = (t + 1 - 2 * core, z)
    tokens, columns = expo.shape
    half = columns // 2
    quarter = half // 2
    group = columns // 8
    part = half // 8
    step_lanes = columns // 16
    plane = 2 * side * side
    block, width = patches_ref.shape

    def wrap(value, n):
        return jnp.where(value >= n, value - n, value)

    at_z, at_q, at_qy, at_x, at_y = {}, {}, {}, {}, {}
    flip = (core, 1 - core)
    for d in range(1, depth):
        at_z[d] = (t, wrap(z + d, depth))
    for d in range(1, 2 * side):
        at_q[d] = (y * (2 * side) + wrap(q + d, 2 * side), z)
        at_qy[d] = ((wrap(y * 2 + core + d, 2 * side) - flip[d % 2]) * side
                    + x * 2 + flip[d % 2], z)
    for d in range(1, side):
        at_x[d] = ((y * side + wrap(x + d, side)) * 2 + core, z)
        at_y[d] = (wrap(y + d, side) * (2 * side) + q, z)

    at_plane = sorted(
        ((min(dy, side - dy) + min(dq, 2 * side - dq) / 2, dy * 2 * side + dq,
          (wrap(y + dy, side) * (2 * side) + wrap(q + dq, 2 * side), z))
         for dy in range(side) for dq in range(2 * side) if dy + dq),
        key=lambda item: (-item[0], item[1]))

    def push(src, dst, send, recv, device):
        copy = pltpu.make_async_remote_copy(
            src_ref=src, dst_ref=dst, send_sem=send, recv_sem=recv,
            device_id=device, device_id_type=MESH,
        )
        copy.start()
        return copy

    def arrived(ref, sem):
        pltpu.make_async_copy(ref, ref, sem).wait()

    def exchange(buf, n, device, send, recv):
        for d in far_first(n):
            push(buf.at[0], buf.at[d], send, recv, device[d])

    def settle(buf, n, recv):
        arrived(buf.at[pl.ds(1, n - 1)], recv)

    loads = [
        pltpu.make_async_copy(src, dst, load_sem.at[i])
        for i, (src, dst) in enumerate((
            (weight_hbm, weight_ref), (patches_hbm, patches_ref), (index_hbm, index_ref)))
    ]
    for load in loads:
        load.start()

    barrier = pltpu.get_barrier_semaphore()
    partners = (
        [at_z[d] for d in (1, 2, depth - 1, depth - 2)]
        + list(at_q.values()) + list(at_qy.values())
    )
    for device in partners:
        pl.semaphore_signal(barrier, inc=1, device_id=device, device_id_type=MESH)

    loads[0].wait()
    square = jnp.sum(weight_ref[...] * weight_ref[...], axis=0, keepdims=True)
    for h in range(2):
        for k in range(8):
            lane = h * half + k * part
            ss_own[h, k:k + 1, :] = square[:, lane:lane + part]
    ss_a[0] = ss_own[core]

    def quarter_of(h, p):
        return pl.ds(pl.multiple_of(h * half + p * quarter, quarter), quarter)

    raw[0, x, core] = weight_ref[:, quarter_of(core, 0)]
    raw[1, y, core] = weight_ref[:, quarter_of(core, 1)]

    loads[1].wait()
    loads[2].wait()
    rows = patches_ref[...].astype(F32)
    norm = lax.rsqrt(jnp.sum(rows * rows, axis=1, keepdims=True) + EPS)
    own = pl.ds(pl.multiple_of(z * block, block), block)
    gathered[own, :] = (rows * norm).astype(BF16)

    pl.semaphore_wait(barrier, len(partners))

    for d in far_first(2 * side):
        push(ss_own.at[flip[d % 2]], ss_a.at[d], ss_send.at[0], ss_recv.at[0], at_q[d])

    reach = (depth // 2, depth - 1 - depth // 2)

    def ring_slot(way, d):
        owner = wrap(z + (depth - d if way == 0 else d), depth)
        return gathered.at[pl.ds(pl.multiple_of(owner * block, block), block)]

    def ring_push(way, d, hops):
        slot = ring_slot(way, d)
        push(slot, slot, ring_send.at[way, d + hops], ring_recv.at[way, d + hops],
             at_z[hops if way == 0 else depth - hops])

    def ring_step(s):
        for way in range(2):
            if s == 0:
                ring_push(way, 0, 2)
                ring_push(way, 0, 1)
        for d in (2 * s - 1, 2 * s):
            for way in range(2):
                if 1 <= d <= reach[way]:
                    arrived(ring_slot(way, d), ring_recv.at[way, d])
                    if d + 2 <= reach[way]:
                        ring_push(way, d, 2)

    ring_steps = depth // 4

    ring_step(0)

    moves = []
    for d in far_first(2 * side):
        moves.append(push(weight_ref.at[:, quarter_of(flip[d % 2], 0)], raw.at[0, x, core],
                          raw_send.at[0, d], raw_recv.at[0, d], at_q[d]))
        moves.append(push(weight_ref.at[:, quarter_of(flip[d % 2], 1)], raw.at[1, y, core],
                          raw_send.at[1, d], raw_recv.at[1, d], at_qy[d]))

    ring_step(1)
    settle(ss_a, 2 * side, ss_recv.at[0])
    ss_y[0] = jnp.sum(ss_a[...], axis=0)
    exchange(ss_y, side, at_y, ss_send.at[1], ss_recv.at[1])
    ring_step(2)
    for d in range(1, 2 * side):
        px = wrap(q - d + 2 * side, 2 * side) // 2
        py = wrap(y * 2 + core - d + 2 * side, 2 * side) // 2
        arrived(raw.at[0, px, flip[d % 2]], raw_recv.at[0, d])
        arrived(raw.at[1, py, flip[d % 2]], raw_recv.at[1, d])
    settle(ss_y, side, ss_recv.at[1])
    inverse = lax.rsqrt(jnp.sum(ss_y[...], axis=0) + EPS)
    for k in range(8):
        p, c, lane = k // 4, (k // 2) % 2, (k % 2) * part
        value = raw[p, :, :, :, (k % 4) * part:(k % 4 + 1) * part].reshape(-1, part)
        value = (value * inverse[k:k + 1, :]).astype(BF16).reshape(side, -1, part)
        if p == 0:
            normed[core, 0, c, y, :, :, lane:lane + part] = value
        else:
            normed[core, 1, c, :, x, :, lane:lane + part] = value

    for c in range(2):
        for d in far_first(side):
            moves.append(push(normed.at[core, 0, c, y], normed.at[core, 0, c, y],
                              n2_send.at[0, c, d], n2_recv.at[0, c, d], at_y[d]))
            moves.append(push(normed.at[core, 1, c, :, x], normed.at[core, 1, c, :, x],
                              n2_send.at[1, c, d], n2_recv.at[1, c, d], at_x[d]))
        if c == 0:
            for s in range(3, ring_steps):
                ring_step(s)

    for j in range(tokens // 128):
        local = (index_ref[j:j + 1, :] - t * (block * depth)).astype(F32)
        column = jnp.broadcast_to(local, (128, 128)).T
        for k in range(block * depth // 128):
            lane = lax.broadcasted_iota(jnp.int32, (128, 128), 1).astype(F32) + 128 * k
            onehot[128 * j:128 * (j + 1), 128 * k:128 * (k + 1)] = jnp.where(
                column == lane, 1.0, 0.0).astype(BF16)

    ring_step(ring_steps)
    features[...] = jnp.dot(onehot[...], gathered[...],
                            preferred_element_type=F32).astype(BF16)

    factor = math.log2(math.e) / TEMP

    def fill(which, c):
        def chunk(i, carry):
            p = i // (group // step_lanes)
            start = pl.multiple_of(lax.rem(i, group // step_lanes) * step_lanes, step_lanes)
            lanes = pl.ds(start, step_lanes)
            weights = normed[which, p, c, :, :, :, lanes].reshape(width, step_lanes)
            row = (which * 4 + p * 2 + c) * (group // step_lanes) + start // step_lanes
            target = pl.ds(pl.multiple_of(row * step_lanes, step_lanes), step_lanes)
            scores = jnp.dot(features[...], weights, preferred_element_type=F32)
            value = jnp.exp2(scores * factor)
            expo[:, target] = value
            total = jnp.sum(value.reshape(tokens // 8, 8, step_lanes), axis=0)
            col_own[pl.ds(row, 1), :] = jnp.sum(total, axis=0, keepdims=True)
            return carry

        lax.fori_loop(0, 2 * (group // step_lanes), chunk, 0)

    def column_push(it):
        col_x[it, 0] = col_own[...].astype(BF16)
        for _, slot, device in at_plane:
            push(col_x.at[it, 0], col_x.at[it, slot], a_send.at[it], a_recv.at[it], device)

    for c in range(2):
        for p in range(2):
            for d in range(1, side):
                if p == 0:
                    block_ref = normed.at[core, 0, c, wrap(y - d + side, side)]
                else:
                    block_ref = normed.at[core, 1, c, :, wrap(x - d + side, side)]
                arrived(block_ref, n2_recv.at[p, c, d])
            moves.append(push(normed.at[core, p, c], normed.at[core, p, c],
                              share_send.at[p, c], share_recv.at[p, c], sibling))
        fill(core, c)
    for c in range(2):
        for p in range(2):
            arrived(normed.at[1 - core, p, c], share_recv.at[p, c])
        fill(1 - core, c)
    column_push(0)

    def columns_to_rows(it, last=False):
        settle(col_x.at[it], plane, a_recv.at[it])
        col_scale[...] = 1.0 / jnp.sum(col_x[it].astype(F32), axis=0)

        def some(g, carry):
            here = pl.ds(pl.multiple_of(g * 64, 64), 64)
            total = jnp.zeros((64, 128), F32)
            for j in range(columns // 128):
                k, l = j // (step_lanes // 128), j % (step_lanes // 128)
                scale = col_scale[k:k + 1, 128 * l:128 * (l + 1)]
                value = expo[here, 128 * j:128 * (j + 1)] * scale
                total += value
                if last:
                    expo[here, 128 * j:128 * (j + 1)] = value
            row_acc[here, :] = total
            return carry

        lax.fori_loop(0, tokens // 64, some, 0)
        for j in range(tokens // 128):
            turned = row_acc[128 * j:128 * (j + 1), :].T
            row_x[it, 0, j:j + 1, :] = jnp.sum(turned, axis=0, keepdims=True)
        exchange(row_x.at[it], depth, at_z, r_send.at[it], r_recv.at[it])

    def rows_to_scale(it):
        settle(row_x.at[it], depth, r_recv.at[it])
        scale = 1.0 / jnp.sum(row_x[it], axis=0)
        for j in range(tokens // 128):
            row_bcast[128 * j:128 * (j + 1), :] = jnp.broadcast_to(
                scale[j:j + 1, :], (128, 128)).T

    def column_pass():
        def chunk(k, carry):
            target = pl.ds(pl.multiple_of(k * group, group), group)
            total = jnp.zeros((8, group), F32)
            for g in range(tokens // 64):
                here = slice(g * 64, (g + 1) * 64)
                scale = jnp.concatenate([row_bcast[here, :]] * (group // 128), axis=1)
                value = expo[here, target] * scale
                total += jnp.sum(value.reshape(8, 8, group), axis=0)
            total = jnp.sum(total, axis=0, keepdims=True)
            for i in range(group // step_lanes):
                col_own[pl.ds(k * (group // step_lanes) + i, 1), :] = (
                    total[:, i * step_lanes:(i + 1) * step_lanes])
            return carry

        lax.fori_loop(0, 8, chunk, 0)

    def sinkhorn(it, carry):
        columns_to_rows(it)
        rows_to_scale(it)
        column_pass()
        column_push(it + 1)
        return carry

    lax.fori_loop(0, ITERS - 1, sinkhorn, 0)
    columns_to_rows(ITERS - 1, last=True)

    for way in range(2):
        for d in range(1, reach[way] + 1):
            arrived(ring_slot(way, d), ring_send.at[way, d])
    for copy in moves:
        copy.wait_send()
    settle(ss_a, 2 * side, ss_send.at[0])
    settle(ss_y, side, ss_send.at[1])
    for it in range(ITERS):
        settle(col_x.at[it], plane, a_send.at[it])
        settle(row_x.at[it], depth, r_send.at[it])

    rows_to_scale(ITERS - 1)


def finish_kernel(scale_out, expo, row_bcast, out_ref, staged, sems):
    tokens, columns = expo.shape
    group = columns // 8
    step = staged.shape[1]
    copies = []
    for g in range(tokens // step):
        here = slice(g * step, (g + 1) * step)
        scale = jnp.concatenate([scale_out * row_bcast[here, :]] * (group // 128), axis=1)
        for k in range(8):
            target = slice(k * group, (k + 1) * group)
            staged[g, :, target] = (expo[here, target] * scale).astype(BF16)
        copies.append(pltpu.make_async_copy(staged.at[g], out_ref.at[pl.ds(g * step, step)],
                                            sems.at[g]))
        copies[-1].start(priority=g % 2)
    for copy in copies:
        copy.wait()


def body(side, depth, patches, mask_index, proto_weight):
    block, width = patches.shape
    tokens = mask_index.shape[0]
    rows, columns = proto_weight.shape
    half, group = columns // 2, columns // 8
    dma = pltpu.SemaphoreType.DMA
    vmem = pl.BlockSpec(memory_space=pltpu.VMEM)
    hbm = pl.BlockSpec(memory_space=pltpu.HBM)
    expo, row_bcast = pl.pallas_call(
        functools.partial(kernel, side, depth),
        out_shape=(
            jax.ShapeDtypeStruct((tokens, columns), F32),
            jax.ShapeDtypeStruct((tokens, 128), F32),
        ),
        in_specs=[hbm] * 3,
        out_specs=(vmem,) * 2,
        scratch_shapes=[
            pltpu.VMEM((block, width), BF16),
            pltpu.VMEM((tokens // 128, 128), jnp.int32),
            pltpu.VMEM((rows, columns), F32),
            pltpu.VMEM((block * depth, width), BF16),
            pltpu.VMEM((tokens, block * depth), BF16),
            pltpu.VMEM((tokens, width), BF16),
            pltpu.VMEM((2, side, 2, rows, half // 2), F32),
            pltpu.VMEM((2, 8, half // 8), F32),
            pltpu.VMEM((2 * side, 8, half // 8), F32),
            pltpu.VMEM((side, 8, half // 8), F32),
            pltpu.VMEM((2, 2, 2, side, side, 2 * rows, group), BF16),
            pltpu.VMEM((tokens, 128), F32),
            pltpu.VMEM((16, columns // 16), F32),
            pltpu.VMEM((16, columns // 16), F32),
            pltpu.VMEM((ITERS, 2 * side * side, 16, columns // 16), BF16),
            pltpu.VMEM((ITERS, depth, tokens // 128, 128), F32),
            dma((3,)),
            dma((2, depth // 2 + 1)), dma((2, depth // 2 + 1)),
            dma((2, 2 * side)), dma((2, 2 * side)),
            dma((2,)), dma((2,)),
            dma((2, 2, side)), dma((2, 2, side)),
            dma((2, 2)), dma((2, 2)),
            dma((ITERS,)), dma((ITERS,)),
            dma((ITERS,)), dma((ITERS,)),
        ],
        compiler_params=pltpu.CompilerParams(
            collective_id=0, has_side_effects=True,
            vmem_limit_bytes=32 * 1024 * 1024,
        ),
        cost_estimate=pl.CostEstimate(
            flops=2 * tokens * columns * width, bytes_accessed=4 * tokens * columns,
            transcendentals=tokens * columns),
    )(*(pltpu.with_memory_space_constraint(v, pltpu.HBM) for v in (
        patches, mask_index.reshape(tokens // 128, 128), proto_weight)))
    step = 32
    return pl.pallas_call(
        functools.partial(finish_kernel, float(columns * depth)),
        out_shape=jax.ShapeDtypeStruct((tokens, columns), BF16),
        in_specs=[vmem] * 2,
        out_specs=hbm,
        scratch_shapes=[pltpu.VMEM((tokens // step, step, columns), BF16),
                        dma((tokens // step,))],
        compiler_params=pltpu.CompilerParams(vmem_limit_bytes=16 * 1024 * 1024),
        cost_estimate=pl.CostEstimate(
            flops=3 * tokens * columns, bytes_accessed=6 * tokens * columns, transcendentals=0),
    )(expo, row_bcast)


def solution(mesh):
    side = math.isqrt(mesh.shape["tok"] // 2)
    return jax.shard_map(
        functools.partial(body, side, mesh.shape["proto"]),
        mesh=mesh,
        in_specs=(P(("tok", "proto"), None), P("tok"), P("tok", "proto")),
        out_specs=P("tok", "proto"),
        check_vma=False,
    )
```
